32 devices in a mesh: groups: 1, dp: 32 (over z, y, x, core).
Axes of the slice: x: 2, y: 2, z: 4, core: 2. Of those that a mesh axis runs over, the one named last changes fastest.
Arguments:
- x_in: bfloat16 [2048, 4096], P('groups', 'dp'), may hold values from -6 to 6
- z_in: bfloat16 [2048, 4096], P('groups', 'dp'), may hold values from -6 to 6
- dt_in: bfloat16 [64, 2048], P('dp', 'groups'), may hold values from -2.5 to 7.5
- bc_in: bfloat16 [8, 2048, 512], P(None, ('groups', 'dp')), may hold values from -6 to 6
- owner_states: float32 [32, 1, 64, 8, 256], P(('groups', 'dp')), may hold values from -1.75 to 1.75
- decay_rate: float32 [64], P('dp'), may hold values from 0.0001 to 1
- dt_bias: float32 [64], P('dp'), may hold values from -4.5 to -2.5
- skip_d: float32 [64], P('dp'), may hold values from 0.5 to 1.5
- norm_gain: float32 [4096], P('dp'), may hold values from 0.5 to 1.5
- owner_map: int32 [4], P('groups'), may hold values from 0 to 3, each once
- prefill_slot: int32 [4], P('groups'), may hold values from 0 to 3, each once
- turn_blocks: int32 [4], P('groups'), may hold values from 1 to 8, 16 in all
Outputs:
- y_out: bfloat16 [2048, 4096], P('groups', 'dp')
- new_owner_states: float32 [32, 1, 64, 8, 256], P(('groups', 'dp'))
The draws below stay inside these ranges and needn't reach their ends.
Inputs may be any that keep to these rules, and one draw needn't show every extreme that they name: `owner_map`: a permutation; slot k belongs to decode owner k. `prefill_slot`: a permutation. `turn_blocks`: sums to 16; a turn of b blocks has b * 128 tokens.
All inputs are finite; a program needn't handle non-finite values.
Results may differ from the reference program's by a relative error of at most 0.0055.
Values may be sent and summed in bfloat16 or wider, within the bound.
A program may use at most 128 MiB of HBM per device.

```python
import math
import jax
import jax.numpy as jnp
import numpy as np
from jax import lax

HEAD_DIM = 64
STATE = 256
NGROUPS = 8
BLOCK_LEN = 128
DEC_TP = 8
OWN_SLOTS = 1
HEADS = 64
PQ = 8
OWNERS = 4
CONVS = 4
MAX_BLOCKS = 8
TOTAL_BLOCKS = 16
ALL_TOKEN_ROWS = 2048
N_DP = 32


def draw_decay_rate(key, part):
    key = jax.random.fold_in(key, 11)
    spread = jax.random.uniform(key, (HEADS,), jnp.float32)
    low_end = 0.001
    high_end = 1.0
    return jnp.exp(jnp.log(low_end) + spread * (jnp.log(high_end) - jnp.log(low_end)))


def draw_dt_in(key, part):
    key = jax.random.fold_in(key, 23)
    noise_key, position_key = jax.random.split(key)
    random_jitter = jnp.clip(0.6 * jax.random.normal(noise_key, (HEADS, ALL_TOKEN_ROWS), jnp.float32), -2.5, 2.5)
    surge_positions = jax.random.randint(position_key, (6,), 0, ALL_TOKEN_ROWS)
    surge_mask = jnp.any(jnp.arange(ALL_TOKEN_ROWS)[None, :] == surge_positions[:, None], axis=0)
    return (random_jitter + 5.0 * surge_mask[None, :].astype(jnp.float32)).astype(jnp.bfloat16)


def block_scale(rng, extent, cuts, least, high):
    gain = 1.0
    for axis_at, parts in cuts:
        steps = jax.random.uniform(jax.random.fold_in(jax.random.fold_in(rng, 6), axis_at), (parts,), jnp.float32, least / len(cuts), high / len(cuts))
        gain = gain * jnp.repeat(jnp.exp(steps), extent[axis_at] // parts).reshape((-1,) + (1,) * (len(extent) - 1 - axis_at))
    return gain


def length_profile(amount, total, most, skew):
    portions = [(1 << 20) // math.isqrt(grade ** skew) + 1 for grade in range(2, amount + 1)]
    surplus, counts = total - most - (amount - 1), [1] * (amount - 1)
    while surplus > 0:
        movable = [i for i in range(amount - 1) if counts[i] < most]
        mass, budget = sum([portions[i] for i in movable]), surplus
        for i in movable:
            more = min(most - counts[i], max(1, budget * portions[i] // mass), surplus)
            counts[i] = counts[i] + more
            surplus = surplus - more
    return np.array([most] + counts)


def ragged_sizes(stream_key, count, total, limit, lean):
    if count == 2:
        one = jax.random.randint(stream_key, (), max(1, total - limit), min(limit, total - 1) + 1)
        return jnp.stack([one, total - one])
    tallies = jnp.asarray(length_profile(count, total, limit, lean), jnp.int32)
    pairs = (count - 1) // 2
    donor, taker = tallies[1:1 + 2 * pairs:2], tallies[2:2 + 2 * pairs:2]
    room = jnp.minimum(donor - 1, limit - taker)
    moved = jax.random.randint(jax.random.fold_in(stream_key, 1), (pairs,), 0, 1 << 20) % (room + 1)
    tallies = tallies.at[1:1 + 2 * pairs:2].set(donor - moved).at[2:2 + 2 * pairs:2].set(taker + moved)
    return tallies[jax.random.permutation(jax.random.fold_in(stream_key, 2), count)]


def normal_values(key, dims, deviation, limit, pieces=(), kind=jnp.bfloat16):
    loudness = block_scale(key, dims, pieces, -0.22, 0.18) if pieces else 1.0
    array = jax.random.normal(key, dims, jnp.float32) * deviation * loudness
    return jnp.minimum(jnp.maximum(array, -limit), limit).astype(kind)


def setup_inputs(seed: int = 0, part: int = 0) -> dict:
    streams_of = jax.random.split(jax.random.key(seed), 13)
    part_keys = jax.random.split(jax.random.fold_in(streams_of[12], part), 13)
    return {
        "x_in": normal_values(part_keys[0], (ALL_TOKEN_ROWS, HEADS * HEAD_DIM), 1.0, 6.0, ((1, 32),)),
        "z_in": normal_values(part_keys[1], (ALL_TOKEN_ROWS, HEADS * HEAD_DIM), 1.0, 6.0, ((1, 32),)),
        "dt_in": draw_dt_in(jax.random.fold_in(jax.random.fold_in(streams_of[12], part), 71), part),
        "bc_in": normal_values(part_keys[3], (NGROUPS, ALL_TOKEN_ROWS, 2 * STATE), 1.0, 6.0, ((1, 32),)),
        "owner_states": normal_values(part_keys[4], (N_DP, OWN_SLOTS, HEADS, PQ, STATE), 0.3, 1.75, ((0, 32),), jnp.float32),
        "decay_rate": draw_decay_rate(jax.random.fold_in(streams_of[12], 71), part),
        "dt_bias": jnp.clip(-4.5 + 2.0 * jax.random.uniform(streams_of[6], (HEADS,), jnp.float32) ** block_scale(streams_of[6], (HEADS,), ((0, 32),), -0.2, 0.2), -4.5, -2.5),
        "skip_d": jnp.clip(0.5 + 1.0 * jax.random.uniform(streams_of[7], (HEADS,), jnp.float32) ** block_scale(streams_of[7], (HEADS,), ((0, 32),), -0.2, 0.2), 0.5, 1.5),
        "norm_gain": jnp.clip(1.0 + 0.1 * jax.random.normal(streams_of[8], (HEADS * HEAD_DIM,), jnp.float32), 0.5, 1.5),
        "owner_map": jax.random.permutation(part_keys[9], CONVS).astype(jnp.int32),
        "prefill_slot": jax.random.permutation(part_keys[10], CONVS).astype(jnp.int32),
        "turn_blocks": ragged_sizes(part_keys[11], CONVS, TOTAL_BLOCKS, MAX_BLOCKS, 2).astype(jnp.int32),
    }


def packing(prefill_slot, turn_blocks, block_total):
    conv_count = turn_blocks.shape[0]
    conv_ids = jnp.arange(conv_count, dtype=jnp.int32)
    before_mask = (prefill_slot[None, :] < prefill_slot[:, None]).astype(jnp.int32)
    first_block = lax.optimization_barrier(jnp.sum(before_mask * turn_blocks[None, :], axis=1)).astype(jnp.int32)
    end_block = (first_block + turn_blocks).astype(jnp.int32)
    block_ids = jnp.arange(block_total, dtype=jnp.int32)
    inside_mask = (block_ids[:, None] >= first_block[None, :]) & (block_ids[:, None] < end_block[None, :])
    block_conv = lax.optimization_barrier(jnp.sum(jnp.where(inside_mask, conv_ids[None, :], 0), axis=1)).astype(jnp.int32)
    return (first_block, end_block, block_conv)

def reference(x_in, z_in, dt_in, bc_in, owner_states, decay_rate, dt_bias, skip_d, norm_gain, owner_map, prefill_slot, turn_blocks):
    first_block, end_block, block_conv = packing(prefill_slot, turn_blocks, TOTAL_BLOCKS)
    block_start = jnp.arange(TOTAL_BLOCKS, dtype=jnp.int32) == first_block[block_conv]
    owner_grid = owner_states.reshape(OWNERS, DEC_TP, OWN_SLOTS, HEADS, PQ, STATE)
    slot_states = jnp.transpose(owner_grid, (0, 2, 3, 1, 4, 5)).reshape(OWNERS * OWN_SLOTS, HEADS, HEAD_DIM, STATE)
    initial = slot_states[owner_map]
    step_size = jax.nn.softplus(dt_in.astype(jnp.float32) + dt_bias[:, None])
    log_decay = -step_size * decay_rate[:, None]
    cum_decay = jnp.cumsum(log_decay.reshape(HEADS, TOTAL_BLOCKS, BLOCK_LEN), axis=2)
    step_blocks = step_size.reshape(HEADS, TOTAL_BLOCKS, BLOCK_LEN)
    b_part = bc_in[:, :, :STATE].astype(jnp.float32).reshape(NGROUPS, TOTAL_BLOCKS, BLOCK_LEN, STATE)
    c_part = bc_in[:, :, STATE:].astype(jnp.float32).reshape(NGROUPS, TOTAL_BLOCKS, BLOCK_LEN, STATE)
    scores = jnp.einsum('gkts,gkus->gktu', c_part, b_part)
    causal = jnp.tril(jnp.ones((BLOCK_LEN, BLOCK_LEN), dtype=bool))
    heads_per_group = HEADS // NGROUPS

    def one_head(head_index):
        group_index = head_index // heads_per_group
        x_head = lax.dynamic_slice_in_dim(x_in, head_index * HEAD_DIM, HEAD_DIM, 1).astype(jnp.float32).reshape(TOTAL_BLOCKS, BLOCK_LEN, HEAD_DIM)
        z_head = lax.dynamic_slice_in_dim(z_in, head_index * HEAD_DIM, HEAD_DIM, 1).astype(jnp.float32).reshape(TOTAL_BLOCKS, BLOCK_LEN, HEAD_DIM)
        cum_head = cum_decay[head_index]
        step_head = step_blocks[head_index]
        score_head = scores[group_index]
        b_head = b_part[group_index]
        c_head = c_part[group_index]
        log_gap = cum_head[:, :, None] - cum_head[:, None, :]
        pair_decay = jnp.exp(jnp.where(causal[None], log_gap, -jnp.inf))
        weights = (score_head * pair_decay * step_head[:, None, :]).astype(jnp.bfloat16)
        local_out = jnp.einsum('ktu,kup->ktp', weights.astype(jnp.float32), x_head)
        block_decay = cum_head[:, -1]
        carried = (x_head * (step_head * jnp.exp(block_decay[:, None] - cum_head))[:, :, None]).astype(jnp.bfloat16)
        block_input = jnp.einsum('kup,kus->kps', carried.astype(jnp.float32), b_head)
        seeds = initial[:, head_index][block_conv]

        def advance(state_prev, inputs):
            overall_decay, added, seed_state, is_start = inputs
            start_state = jnp.where(is_start, seed_state, state_prev)
            end_state = jnp.exp(overall_decay) * start_state + added
            return (end_state, (start_state, end_state))
        empty_state = jnp.zeros((HEAD_DIM, STATE), jnp.float32)
        _, (starts, ends) = lax.scan(advance, empty_state, (block_decay, block_input, seeds, block_start))
        final_head = ends[end_block - 1]
        state_out = jnp.exp(cum_head)[:, :, None] * jnp.einsum('kts,kps->ktp', c_head, starts, precision=lax.Precision.HIGHEST)
        mixer_out = local_out + state_out + skip_d[head_index] * x_head
        gated = mixer_out * jax.nn.silu(z_head)
        return (gated.reshape(ALL_TOKEN_ROWS, HEAD_DIM), final_head)
    gated_all, finals = lax.map(one_head, jnp.arange(HEADS, dtype=jnp.int32))
    grouped = gated_all.reshape(NGROUPS, heads_per_group, ALL_TOKEN_ROWS, HEAD_DIM)
    mean_sq = lax.optimization_barrier(jnp.mean(grouped * grouped, axis=(1, 3)))
    normed = grouped * lax.rsqrt(mean_sq[:, None, :, None] + 1e-05)
    mixed = jnp.transpose(normed.reshape(HEADS, ALL_TOKEN_ROWS, HEAD_DIM), (1, 0, 2)).reshape(ALL_TOKEN_ROWS, HEADS * HEAD_DIM)
    y_out = (mixed * norm_gain[None, :]).astype(jnp.bfloat16)
    new_slots = slot_states.at[owner_map].set(jnp.transpose(finals, (1, 0, 2, 3)))
    new_owner = jnp.transpose(new_slots.reshape(OWNERS, OWN_SLOTS, HEADS, DEC_TP, PQ, STATE), (0, 3, 1, 2, 4, 5)).reshape(N_DP, OWN_SLOTS, HEADS, PQ, STATE)
    return (y_out, new_owner)
```

```python
import functools

import jax
import jax.numpy as jnp
from jax import lax
from jax.experimental import pallas as pl
from jax.experimental.pallas import tpu as pltpu
from jax.sharding import PartitionSpec as P

BLOCK_LEN = 128


exact_mode = lax.Precision.HIGHEST


def shortened(x):

    def short(part):
        return part.astype(jnp.bfloat16) if part.dtype == jnp.float32 else part

    return jax.tree.map(short, x)


def from_partner(x, axis, bit):
    return lax.ppermute(x, axis, [(i, i ^ 1 << bit) for i in range(lax.axis_size(axis))])


def packing(prefill_slot, turn_blocks, block_total):
    conv_count = turn_blocks.shape[0]
    conv_ids = jnp.arange(conv_count, dtype=jnp.int32)
    before_mask = (prefill_slot[None, :] < prefill_slot[:, None]).astype(jnp.int32)
    first_block = jnp.sum(before_mask * turn_blocks[None, :], axis=1)
    end_block = first_block + turn_blocks
    block_ids = jnp.arange(block_total, dtype=jnp.int32)
    inside_mask = (block_ids[:, None] >= first_block[None, :]) & (
        block_ids[:, None] < end_block[None, :]
    )
    block_conv = jnp.sum(jnp.where(inside_mask, conv_ids[None, :], 0), axis=1)
    return (first_block, end_block, block_conv)


def fetch_states(owner_states):
    return lax.all_to_all(
        owner_states[0].astype(jnp.bfloat16), "dp", split_axis=1, concat_axis=2, tiled=True
    ).astype(jnp.float32)


def shards(
    x_in,
    z_in,
    dt_in,
    bc_in,
    owner_states,
    decay_rate,
    dt_bias,
    skip_d,
    norm_gain,
    owner_map,
    prefill_slot,
    turn_blocks,
):
    device_count = lax.axis_size("dp")
    token_count = x_in.shape[0]
    head_local = dt_in.shape[0]
    head_width = x_in.shape[1] // head_local
    group_count = bc_in.shape[0]
    state_width = bc_in.shape[2] // 2
    slot_count = owner_states.shape[1]
    channel_part = owner_states.shape[3]
    decode_width = head_width // channel_part
    owner_count = device_count // decode_width
    block_count = token_count // BLOCK_LEN
    conv_count = owner_map.shape[0]
    per_group = device_count // group_count
    first_block, end_block, block_conv = packing(prefill_slot, turn_blocks, block_count)
    slot_of = owner_map % slot_count
    owner_of = owner_map // slot_count
    copies = jnp.repeat(bc_in, per_group, axis=0)
    bc_group = lax.all_to_all(copies, "dp", split_axis=0, concat_axis=1, tiled=True)[0]
    b_part = bc_group[:, :state_width].reshape(block_count, BLOCK_LEN, state_width)
    c_part = bc_group[:, state_width:].reshape(block_count, BLOCK_LEN, state_width)
    c_float = c_part.astype(jnp.float32)
    step_size = jax.nn.softplus(dt_in.astype(jnp.float32) + dt_bias[:, None])
    log_decay = -step_size * decay_rate[:, None]
    cum_decay = jnp.cumsum(log_decay.reshape(head_local, block_count, BLOCK_LEN), axis=2)
    step_blocks = step_size.reshape(head_local, block_count, BLOCK_LEN)
    block_decay = cum_decay[:, :, -1]
    value_blocks = x_in.reshape(block_count, BLOCK_LEN, head_local, head_width)
    gate_blocks = z_in.reshape(block_count, BLOCK_LEN, head_local, head_width)
    scores = jnp.einsum("kts,kus->ktu", c_part, b_part, preferred_element_type=jnp.float32)
    causal = jnp.arange(BLOCK_LEN)[:, None] >= jnp.arange(BLOCK_LEN)[None, :]
    log_gap = cum_decay[:, :, :, None] - cum_decay[:, :, None, :]
    pair_decay = jnp.exp(jnp.where(causal[None, None], log_gap, -jnp.inf))
    weights = (scores[None] * pair_decay * step_blocks[:, :, None, :]).astype(jnp.bfloat16)
    local_out = jnp.einsum(
        "hktu,kuhp->kthp", weights, value_blocks, preferred_element_type=jnp.float32
    )
    tail_scale = jnp.transpose(
        step_blocks * jnp.exp(block_decay[:, :, None] - cum_decay), (1, 2, 0)
    )
    carried = (value_blocks * tail_scale[..., None]).astype(jnp.bfloat16)
    block_input = jnp.einsum("kuhp,kus->khps", carried, b_part, preferred_element_type=jnp.float32)
    block_ids = jnp.arange(block_count, dtype=jnp.int32)
    target_end = jnp.concatenate([block_ids, end_block])
    target_conv = jnp.concatenate([block_conv, jnp.arange(conv_count, dtype=jnp.int32)])
    destination_first = first_block[target_conv]
    link_mask = (block_conv[None, :] == target_conv[:, None]) & (
        block_ids[None, :] < target_end[:, None]
    )
    lead_sum = jnp.concatenate(
        [jnp.zeros((head_local, 1), jnp.float32), jnp.cumsum(block_decay, axis=1)], axis=1
    )
    lead_end = lead_sum[:, target_end]
    carry_weight = jnp.exp(
        jnp.where(link_mask[None], lead_end[:, :, None] - lead_sum[:, None, 1:], -jnp.inf)
    )
    seed_weight = jnp.exp(lead_end - lead_sum[:, destination_first])
    zero_part = jnp.einsum("hrj,jhps->rhps", carry_weight, block_input, precision=exact_mode)
    decay_factor = jnp.transpose(jnp.exp(cum_decay), (1, 2, 0))[..., None]
    shaped = fetch_states(owner_states).reshape(
        slot_count, head_local, owner_count, head_width, state_width
    )
    initial = shaped[slot_of, :, owner_of]
    boundary = zero_part + jnp.transpose(seed_weight)[:, :, None, None] * initial[target_conv]
    state_out = decay_factor * jnp.einsum(
        "kts,khps->kthp", c_float, boundary[:block_count], precision=exact_mode
    )
    final_state = boundary[block_count:]
    mixer_out = local_out + state_out + skip_d[None, None, :, None] * value_blocks
    gated = mixer_out * jax.nn.silu(gate_blocks.astype(jnp.float32))
    gated_rows = gated.reshape(token_count, head_local * head_width)
    part_square = jnp.sum(gated_rows * gated_rows, axis=1)
    group_square = part_square
    for bit_index in range(per_group.bit_length() - 1):
        group_square = group_square + from_partner(shortened(group_square), "dp", bit_index).astype(
            group_square.dtype
        )
    mean_square = group_square / (per_group * head_local * head_width)
    y_out = (gated_rows * lax.rsqrt(mean_square + 1e-05)[:, None] * norm_gain[None, :]).astype(
        jnp.bfloat16
    )
    blank_slots = jnp.zeros(
        (slot_count, head_local, owner_count, head_width, state_width), jnp.float32
    )
    filled = blank_slots.at[slot_of, :, owner_of].set(final_state)
    outgoing = filled.reshape(slot_count, head_local, owner_count * head_width, state_width)
    returned = lax.all_to_all(outgoing, "dp", split_axis=2, concat_axis=1, tiled=True)
    return (y_out, returned[None])


def lanes_dot(a, b):
    return lax.dot_general(a, b, (((1,), (1,)), ((), ())), preferred_element_type=jnp.float32)


def rows_dot(a, b):
    return lax.dot_general(a, b, (((0,), (0,)), ((), ())), preferred_element_type=jnp.float32)


def layer_kernel(
    devices,
    blocks,
    owners,
    om_ref,
    ps_ref,
    tb_ref,
    bias_ref,
    rate_ref,
    skip_ref,
    x_ref,
    z_ref,
    dt_ref,
    bc_ref,
    st_ref,
    gain_ref,
    y_ref,
    ns_ref,
    b_buf,
    c_buf,
    s_out,
    s_in,
    f_out,
    f_in,
    sq_out,
    sq_in,
    seeds,
    pair,
    grow,
    added,
    starts,
    carried,
    gated,
    rows_scr,
    cols_scr,
    edge_scr,
    near_send,
    near_recv,
    side_send,
    side_recv,
    twin_send,
    twin_recv,
    last_send,
    last_recv,
    init_send,
    init_recv,
    fin_send,
    fin_recv,
    sq_send,
    sq_recv,
):
    me = lax.axis_index("dp")
    L = BLOCK_LEN
    quads = devices // 4
    quad = me // 4
    spot = me % 4
    twin = me + 1 - 2 * (me % 2)
    side = me + 2 - 4 * ((me // 2) % 2)
    twin_spot, side_spot = twin % 4, side % 4
    diag_spot = 3 - spot
    width = b_buf.shape[1]
    bufs = (b_buf, c_buf)
    tokens = bc_ref.shape[1]

    def remote(src, dst, send, recv, to):
        return pltpu.make_async_remote_copy(
            src_ref=src,
            dst_ref=dst,
            send_sem=send,
            recv_sem=recv,
            device_id={"dp": to},
            device_id_type=pl.DeviceIdType.MESH,
        )

    def chunk(k, q, s):
        return bufs[k].at[pl.ds(pl.multiple_of((4 * q + s) * tokens, tokens), tokens), :]

    def near(k, q):
        return remote(
            bc_ref.at[q, :, k * width : (k + 1) * width],
            chunk(k, quad, spot),
            near_send.at[k, q],
            near_recv.at[k, quad],
            4 * q + spot,
        )

    def near_in(k, q):
        return remote(
            chunk(k, q, spot), chunk(k, q, spot), near_send.at[k, q], near_recv.at[k, q], side
        )

    def to_side(k, q, s):
        return remote(chunk(k, q, s), chunk(k, q, s), side_send.at[k, q], side_recv.at[k, q], side)

    def to_twin(k, q, s):
        return remote(chunk(k, q, s), chunk(k, q, s), twin_send.at[k, q], twin_recv.at[k, q], twin)

    def to_twin_last(k, q, s):
        return remote(chunk(k, q, s), chunk(k, q, s), last_send.at[k, q], last_recv.at[k, q], twin)

    def init_copy(d):
        return remote(s_out.at[d], s_in.at[me], init_send.at[d], init_recv.at[me], d)

    def init_from(d):
        return remote(s_in.at[d], s_in.at[d], init_send.at[d], init_recv.at[d], side)

    def fin_copy(d):
        return remote(f_out.at[d], f_in.at[me], fin_send.at[d], fin_recv.at[me], d)

    def fin_from(d):
        return remote(f_in.at[d], f_in.at[d], fin_send.at[d], fin_recv.at[d], side)

    def every(count, body):
        lax.fori_loop(0, count, lambda i, c: (body(i), c)[1], 0)

    barrier = pltpu.get_barrier_semaphore()

    def greet(i):
        pl.semaphore_signal(
            barrier,
            inc=1,
            device_id={"dp": (me + 1 + i) % devices},
            device_id_type=pl.DeviceIdType.MESH,
        )

    every(devices - 1, greet)

    def narrow(d):
        s_out[d] = st_ref[pl.ds(pl.multiple_of(d * 16, 16), 16), :].astype(jnp.bfloat16)

    every(devices, narrow)
    pl.semaphore_wait(barrier, devices - 1)

    def send_near(k):
        every(quads - 1, lambda i: near(k, (quad + 1 + i) % quads).start())

    send_near(0)
    every(devices - 1, lambda i: init_copy((me + 1 + i) % devices).start())
    send_near(1)
    mine = pl.ds(pl.multiple_of(me * tokens, tokens), tokens)
    b_buf[mine, :] = bc_ref[quad, :, :width]
    c_buf[mine, :] = bc_ref[quad, :, width:]
    s_in[me] = s_out[me]

    wide = dt_ref[...].astype(jnp.float32)
    for j in range(blocks):
        rows_scr[2 * j : 2 * j + 2, :] = wide[:, j * L : (j + 1) * L]
    row = lax.broadcasted_iota(jnp.int32, (2 * blocks, L), 0)
    lane = lax.broadcasted_iota(jnp.int32, (2 * blocks, L), 1)
    first_head = row % 2 == 0
    raw = rows_scr[0 : 2 * blocks, :] + jnp.where(first_head, bias_ref[0], bias_ref[1])
    step = jnp.maximum(raw, 0.0) + jnp.log1p(jnp.exp(-jnp.abs(raw)))
    cum = -step * jnp.where(first_head, rate_ref[0], rate_ref[1])
    shift = 1
    while shift < L:
        cum = cum + jnp.where(lane >= shift, pltpu.roll(cum, shift, 1), 0.0)
        shift *= 2
    total = cum[:, L - 1 : L]
    tail = step * jnp.exp(total - cum)
    growth = jnp.exp(cum)
    rows_scr[0 : 2 * blocks, :] = cum
    rows_scr[2 * blocks : 4 * blocks, :] = step
    edge_scr[...] = jnp.broadcast_to(jnp.exp(total), (2 * blocks, L))
    stacked = jnp.concatenate([cum, tail, growth, step], axis=0)
    cols_scr[...] = jnp.transpose(stacked)

    square_row = lax.broadcasted_iota(jnp.int32, (L, L), 0)
    square_lane = lax.broadcasted_iota(jnp.int32, (L, L), 1)
    causal = square_row >= square_lane
    half = square_lane < L // 2
    gap = 2 * blocks

    def rows_of(j):
        return pl.ds(pl.multiple_of(j * L, L), L)

    def prepare(j):
        turned = pltpu.roll(cols_scr[...], (L - 2 * j) % L, 1)

        def spread(at):
            return jnp.where(half, turned[:, at : at + 1], turned[:, at + 1 : at + 2])

        carried[rows_of(j), :] = (
            x_ref[rows_of(j), :].astype(jnp.float32) * spread(gap)
        ).astype(jnp.bfloat16)
        grow[j] = spread(2 * gap)
        for h in range(2):
            cum_row = rows_scr[pl.ds(2 * j + h, 1), :]
            step_row = rows_scr[pl.ds(gap + 2 * j + h, 1), :]
            log_gap = turned[:, h : h + 1] - cum_row
            pair[2 * j + h] = jnp.exp(jnp.where(causal, log_gap, -jnp.inf)) * step_row

    every(blocks, prepare)

    def gather(k, work):
        def turn(i):
            @pl.when(i < quads)
            def _():
                q = (quad - i + quads) % quads

                @pl.when(i > 0)
                def _():
                    near_in(k, q).wait_recv()

                to_side(k, q, spot).start()
                to_twin(k, q, spot).start()

            @pl.when((i >= 1) & (i < quads + 1))
            def _():
                q = (quad - i + 1 + quads) % quads
                to_side(k, q, side_spot).wait_recv()
                to_twin_last(k, q, side_spot).start()

            @pl.when(i >= 2)
            def _():
                q = (quad - i + 2 + quads) % quads
                to_twin(k, q, twin_spot).wait_recv()
                to_twin_last(k, q, diag_spot).wait_recv()
                work(2 * q)
                work(2 * q + 1)

        every(quads + 2, turn)

    def add_block(j):
        added[j] = rows_dot(carried[rows_of(j), :], b_buf[rows_of(j), :])

    gather(0, add_block)

    every(devices - 1, lambda i: init_from((me + 1 + i) % devices).wait_recv())
    for k in range(owners):
        for q in range(8):
            piece = s_in[8 * k + q].astype(jnp.float32)
            seeds[k, 8 * q : 8 * q + 8, :] = piece[0:8]
            seeds[k, 64 + 8 * q : 72 + 8 * q, :] = piece[8:16]

    first = [
        sum(
            jnp.where(ps_ref[d] < ps_ref[c], tb_ref[d], 0) for d in range(owners)
        )
        for c in range(owners)
    ]
    end = [first[c] + tb_ref[c] for c in range(owners)]
    state_row = lax.broadcasted_iota(jnp.int32, (L, width), 0)

    def advance(j, state):
        is_start = sum(jnp.where(first[c] == j, 1, 0) for c in range(owners))
        owner = sum(
            jnp.where((first[c] <= j) & (j < end[c]), om_ref[c], 0) for c in range(owners)
        )
        owner = jnp.clip(owner, 0, owners - 1)
        start = jnp.where(is_start > 0, seeds[owner], state)
        starts[j] = start.astype(jnp.bfloat16)
        decay = jnp.where(
            state_row < L // 2,
            edge_scr[pl.ds(2 * j, 1), 0:1],
            edge_scr[pl.ds(2 * j + 1, 1), 0:1],
        )
        after = decay * start + added[j]
        added[j] = after
        return after

    lax.fori_loop(0, blocks, advance, jnp.zeros((L, width), jnp.float32))

    for k in range(owners):
        last = sum(jnp.where(om_ref[c] == k, end[c] - 1, 0) for c in range(owners))
        done = added[jnp.clip(last, 0, blocks - 1)]
        for q in range(8):
            f_out[8 * k + q] = jnp.concatenate(
                [done[8 * q : 8 * q + 8], done[64 + 8 * q : 72 + 8 * q]], axis=0
            ).astype(jnp.bfloat16)
    every(devices - 1, lambda i: fin_copy((me + 1 + i) % devices).start())
    f_in[me] = f_out[me]

    skip_lane = jnp.where(square_lane[0:1] < L // 2, skip_ref[0], skip_ref[1])
    cols_scr[...] = jnp.zeros((L, L), jnp.float32)

    def out_block(j):
        rows = rows_of(j)
        c_block = c_buf[rows, :]
        x_block = x_ref[rows, :]
        scores = lanes_dot(c_block, b_buf[rows, :])
        parts = [
            jnp.dot(
                (scores * pair[2 * j + h]).astype(jnp.bfloat16),
                x_block,
                preferred_element_type=jnp.float32,
            )
            for h in range(2)
        ]
        from_state = grow[j] * lanes_dot(c_block, starts[j])
        mixed = (
            jnp.where(half, parts[0], parts[1])
            + from_state
            + skip_lane * x_block.astype(jnp.float32)
        )
        z_block = z_ref[rows, :].astype(jnp.float32)
        result = mixed * (z_block / (1.0 + jnp.exp(-z_block)))
        gated[rows, :] = result
        total_square = jnp.sum(result * result, axis=1, keepdims=True)
        cols_scr[...] = jnp.where(square_lane == j, total_square, cols_scr[...])

    gather(1, out_block)

    sq_out[...] = jnp.transpose(cols_scr[...])[0:blocks]

    def sq_copy(i):
        other = (spot + 1 + i) % 4
        return remote(sq_out, sq_in.at[spot], sq_send.at[other], sq_recv.at[spot], 4 * quad + other)

    def sq_from(i):
        other = (spot + 1 + i) % 4
        return remote(sq_out, sq_in.at[other], sq_send.at[other], sq_recv.at[other], side)

    every(3, lambda i: sq_copy(i).start())
    sq_in[spot] = sq_out[...]
    every(devices - 1, lambda i: fin_from((me + 1 + i) % devices).wait_recv())

    def widen(d):
        ns_ref[pl.ds(pl.multiple_of(d * 16, 16), 16), :] = f_in[d].astype(jnp.float32)

    every(devices, widen)
    every(3, lambda i: sq_from(i).wait_recv())
    group_square = (sq_in[0] + sq_in[1]) + (sq_in[2] + sq_in[3])
    inverse = lax.rsqrt(group_square / (4 * L) + 1e-05)
    cols_scr[...] = jnp.transpose(
        jnp.concatenate([inverse, jnp.zeros((L - blocks, L), jnp.float32)], axis=0)
    )
    gain = gain_ref[...]

    def norm_block(j):
        turned = pltpu.roll(cols_scr[...], (L - j) % L, 1)
        y_ref[rows_of(j), :] = (gated[rows_of(j), :] * turned[:, 0:1] * gain).astype(jnp.bfloat16)

    every(blocks, norm_block)

    def drain(q):
        for k in range(2):

            @pl.when(q != quad)
            def _():
                near(k, q).wait_send()

            to_side(k, q, spot).wait_send()
            to_twin(k, q, spot).wait_send()
            to_twin_last(k, q, side_spot).wait_send()

    every(quads, drain)

    def drain_states(i):
        d = (me + 1 + i) % devices
        init_copy(d).wait_send()
        fin_copy(d).wait_send()

    every(devices - 1, drain_states)
    every(3, lambda i: sq_copy(i).wait_send())


def fused(
    x_in,
    z_in,
    dt_in,
    bc_in,
    owner_states,
    decay_rate,
    dt_bias,
    skip_d,
    norm_gain,
    owner_map,
    prefill_slot,
    turn_blocks,
):
    devices = lax.axis_size("dp")
    tokens, columns = x_in.shape
    blocks = tokens // BLOCK_LEN
    owners = owner_map.shape[0]
    state = bc_in.shape[2] // 2
    quads = devices // 4
    vmem = pl.BlockSpec(memory_space=pltpu.VMEM)
    smem = pl.BlockSpec(memory_space=pltpu.SMEM)
    f32, bf16 = jnp.float32, jnp.bfloat16
    L = BLOCK_LEN
    dma = pltpu.SemaphoreType.DMA
    y_out, new_states = pl.pallas_call(
        functools.partial(layer_kernel, devices, blocks, owners),
        out_shape=(
            jax.ShapeDtypeStruct((tokens, columns), bf16),
            jax.ShapeDtypeStruct((devices * 16, state), f32),
        ),
        in_specs=[smem] * 6 + [vmem] * 6,
        out_specs=(vmem, vmem),
        scratch_shapes=[
            pltpu.VMEM((tokens, state), bf16),
            pltpu.VMEM((tokens, state), bf16),
            pltpu.VMEM((devices, 16, state), bf16),
            pltpu.VMEM((devices, 16, state), bf16),
            pltpu.VMEM((devices, 16, state), bf16),
            pltpu.VMEM((devices, 16, state), bf16),
            pltpu.VMEM((blocks, L), f32),
            pltpu.VMEM((4, blocks, L), f32),
            pltpu.VMEM((owners, L, state), f32),
            pltpu.VMEM((2 * blocks, L, L), f32),
            pltpu.VMEM((blocks, L, L), f32),
            pltpu.VMEM((blocks, L, state), f32),
            pltpu.VMEM((blocks, L, state), bf16),
            pltpu.VMEM((tokens, columns), bf16),
            pltpu.VMEM((tokens, columns), f32),
            pltpu.VMEM((4 * blocks, L), f32),
            pltpu.VMEM((L, L), f32),
            pltpu.VMEM((2 * blocks, L), f32),
        ]
        + [dma((2, quads))] * 8
        + [dma((devices,))] * 4
        + [dma((4,))] * 2,
        compiler_params=pltpu.CompilerParams(
            collective_id=0, has_side_effects=True, vmem_limit_bytes=40 * 1024 * 1024
        ),
    )(
        owner_map,
        prefill_slot,
        turn_blocks,
        dt_bias,
        decay_rate,
        skip_d,
        x_in,
        z_in,
        dt_in,
        bc_in,
        owner_states.reshape(-1, state),
        norm_gain.reshape(1, columns),
    )
    return (y_out, new_states.reshape(owner_states.shape))


def choose(*arrays):
    x_in, dt_in, bc_in, owner_states, owner_map = (arrays[i] for i in (0, 2, 3, 4, 9))
    devices = lax.axis_size("dp")
    fits = (
        devices == 4 * bc_in.shape[0]
        and x_in.shape[0] == 16 * BLOCK_LEN
        and x_in.shape[1] == BLOCK_LEN
        and dt_in.shape[0] == 2
        and owner_states.shape[1] == 1
        and owner_states.shape[3] == 8
        and devices == 8 * owner_map.shape[0]
    )
    return (fused if fits else shards)(*arrays)


def solution(mesh):
    placed = (
        P("groups", "dp"),
        P("groups", "dp"),
        P("dp", "groups"),
        P(None, ("groups", "dp"), None),
        P(("groups", "dp"), None, None, None, None),
        P("dp"),
        P("dp"),
        P("dp"),
        P("dp"),
        P("groups"),
        P("groups"),
        P("groups"),
    )
    return jax.shard_map(
        choose,
        mesh=mesh,
        in_specs=placed,
        out_specs=(P("groups", "dp"), P(("groups", "dp"), None, None, None, None)),
        check_vma=False,
    )
```

```python
import functools

import jax
import jax.numpy as jnp
from jax import lax
from jax.experimental import pallas as pl
from jax.experimental.pallas import tpu as pltpu
from jax.sharding import PartitionSpec as P

BLOCK_LEN = 128


exact_mode = lax.Precision.HIGHEST


def shortened(x):

    def short(part):
        return part.astype(jnp.bfloat16) if part.dtype == jnp.float32 else part

    return jax.tree.map(short, x)


def from_partner(x, axis, bit):
    return lax.ppermute(x, axis, [(i, i ^ 1 << bit) for i in range(lax.axis_size(axis))])


def packing(prefill_slot, turn_blocks, block_total):
    conv_count = turn_blocks.shape[0]
    conv_ids = jnp.arange(conv_count, dtype=jnp.int32)
    before_mask = (prefill_slot[None, :] < prefill_slot[:, None]).astype(jnp.int32)
    first_block = jnp.sum(before_mask * turn_blocks[None, :], axis=1)
    end_block = first_block + turn_blocks
    block_ids = jnp.arange(block_total, dtype=jnp.int32)
    inside_mask = (block_ids[:, None] >= first_block[None, :]) & (
        block_ids[:, None] < end_block[None, :]
    )
    block_conv = jnp.sum(jnp.where(inside_mask, conv_ids[None, :], 0), axis=1)
    return (first_block, end_block, block_conv)


def fetch_states(owner_states):
    return lax.all_to_all(
        owner_states[0].astype(jnp.bfloat16), "dp", split_axis=1, concat_axis=2, tiled=True
    ).astype(jnp.float32)


def shards(
    x_in,
    z_in,
    dt_in,
    bc_in,
    owner_states,
    decay_rate,
    dt_bias,
    skip_d,
    norm_gain,
    owner_map,
    prefill_slot,
    turn_blocks,
):
    device_count = lax.axis_size("dp")
    token_count = x_in.shape[0]
    head_local = dt_in.shape[0]
    head_width = x_in.shape[1] // head_local
    group_count = bc_in.shape[0]
    state_width = bc_in.shape[2] // 2
    slot_count = owner_states.shape[1]
    channel_part = owner_states.shape[3]
    decode_width = head_width // channel_part
    owner_count = device_count // decode_width
    block_count = token_count // BLOCK_LEN
    conv_count = owner_map.shape[0]
    per_group = device_count // group_count
    first_block, end_block, block_conv = packing(prefill_slot, turn_blocks, block_count)
    slot_of = owner_map % slot_count
    owner_of = owner_map // slot_count
    copies = jnp.repeat(bc_in, per_group, axis=0)
    bc_group = lax.all_to_all(copies, "dp", split_axis=0, concat_axis=1, tiled=True)[0]
    b_part = bc_group[:, :state_width].reshape(block_count, BLOCK_LEN, state_width)
    c_part = bc_group[:, state_width:].reshape(block_count, BLOCK_LEN, state_width)
    c_float = c_part.astype(jnp.float32)
    step_size = jax.nn.softplus(dt_in.astype(jnp.float32) + dt_bias[:, None])
    log_decay = -step_size * decay_rate[:, None]
    cum_decay = jnp.cumsum(log_decay.reshape(head_local, block_count, BLOCK_LEN), axis=2)
    step_blocks = step_size.reshape(head_local, block_count, BLOCK_LEN)
    block_decay = cum_decay[:, :, -1]
    value_blocks = x_in.reshape(block_count, BLOCK_LEN, head_local, head_width)
    gate_blocks = z_in.reshape(block_count, BLOCK_LEN, head_local, head_width)
    scores = jnp.einsum("kts,kus->ktu", c_part, b_part, preferred_element_type=jnp.float32)
    causal = jnp.arange(BLOCK_LEN)[:, None] >= jnp.arange(BLOCK_LEN)[None, :]
    log_gap = cum_decay[:, :, :, None] - cum_decay[:, :, None, :]
    pair_decay = jnp.exp(jnp.where(causal[None, None], log_gap, -jnp.inf))
    weights = (scores[None] * pair_decay * step_blocks[:, :, None, :]).astype(jnp.bfloat16)
    local_out = jnp.einsum(
        "hktu,kuhp->kthp", weights, value_blocks, preferred_element_type=jnp.float32
    )
    tail_scale = jnp.transpose(
        step_blocks * jnp.exp(block_decay[:, :, None] - cum_decay), (1, 2, 0)
    )
    carried = (value_blocks * tail_scale[..., None]).astype(jnp.bfloat16)
    block_input = jnp.einsum("kuhp,kus->khps", carried, b_part, preferred_element_type=jnp.float32)
    block_ids = jnp.arange(block_count, dtype=jnp.int32)
    target_end = jnp.concatenate([block_ids, end_block])
    target_conv = jnp.concatenate([block_conv, jnp.arange(conv_count, dtype=jnp.int32)])
    destination_first = first_block[target_conv]
    link_mask = (block_conv[None, :] == target_conv[:, None]) & (
        block_ids[None, :] < target_end[:, None]
    )
    lead_sum = jnp.concatenate(
        [jnp.zeros((head_local, 1), jnp.float32), jnp.cumsum(block_decay, axis=1)], axis=1
    )
    lead_end = lead_sum[:, target_end]
    carry_weight = jnp.exp(
        jnp.where(link_mask[None], lead_end[:, :, None] - lead_sum[:, None, 1:], -jnp.inf)
    )
    seed_weight = jnp.exp(lead_end - lead_sum[:, destination_first])
    zero_part = jnp.einsum("hrj,jhps->rhps", carry_weight, block_input, precision=exact_mode)
    decay_factor = jnp.transpose(jnp.exp(cum_decay), (1, 2, 0))[..., None]
    shaped = fetch_states(owner_states).reshape(
        slot_count, head_local, owner_count, head_width, state_width
    )
    initial = shaped[slot_of, :, owner_of]
    boundary = zero_part + jnp.transpose(seed_weight)[:, :, None, None] * initial[target_conv]
    state_out = decay_factor * jnp.einsum(
        "kts,khps->kthp", c_float, boundary[:block_count], precision=exact_mode
    )
    final_state = boundary[block_count:]
    mixer_out = local_out + state_out + skip_d[None, None, :, None] * value_blocks
    gated = mixer_out * jax.nn.silu(gate_blocks.astype(jnp.float32))
    gated_rows = gated.reshape(token_count, head_local * head_width)
    part_square = jnp.sum(gated_rows * gated_rows, axis=1)
    group_square = part_square
    for bit_index in range(per_group.bit_length() - 1):
        group_square = group_square + from_partner(shortened(group_square), "dp", bit_index).astype(
            group_square.dtype
        )
    mean_square = group_square / (per_group * head_local * head_width)
    y_out = (gated_rows * lax.rsqrt(mean_square + 1e-05)[:, None] * norm_gain[None, :]).astype(
        jnp.bfloat16
    )
    blank_slots = jnp.zeros(
        (slot_count, head_local, owner_count, head_width, state_width), jnp.float32
    )
    filled = blank_slots.at[slot_of, :, owner_of].set(final_state)
    outgoing = filled.reshape(slot_count, head_local, owner_count * head_width, state_width)
    returned = lax.all_to_all(outgoing, "dp", split_axis=2, concat_axis=1, tiled=True)
    return (y_out, returned[None])


def lanes_dot(a, b):
    return lax.dot_general(a, b, (((1,), (1,)), ((), ())), preferred_element_type=jnp.float32)


def rows_dot(a, b):
    return lax.dot_general(a, b, (((0,), (0,)), ((), ())), preferred_element_type=jnp.float32)


def layer_kernel(
    devices,
    blocks,
    owners,
    om_ref,
    ps_ref,
    tb_ref,
    bias_ref,
    rate_ref,
    skip_ref,
    dt_ref,
    gain_ref,
    x_hbm,
    z_hbm,
    bc_ref,
    st_hbm,
    y_ref,
    ns_ref,
    x_ref,
    z_ref,
    st_ref,
    b_buf,
    c_buf,
    s_out,
    s_in,
    f_out,
    f_in,
    sq_out,
    sq_in,
    seeds,
    pair,
    grow,
    added,
    starts,
    carried,
    gated,
    rows_scr,
    cols_scr,
    edge_scr,
    near_send,
    near_recv,
    side_send,
    side_recv,
    twin_send,
    twin_recv,
    last_send,
    last_recv,
    init_send,
    init_recv,
    fin_send,
    fin_recv,
    sq_send,
    sq_recv,
    load_sem,
):
    me = lax.axis_index("dp")
    L = BLOCK_LEN
    quads = devices // 4
    quad = me // 4
    spot = me % 4
    twin = me + 1 - 2 * (me % 2)
    side = me + 2 - 4 * ((me // 2) % 2)
    twin_spot, side_spot = twin % 4, side % 4
    diag_spot = 3 - spot
    width = b_buf.shape[1]
    bufs = (b_buf, c_buf)
    tokens = bc_ref.shape[1]

    def remote(src, dst, send, recv, to):
        return pltpu.make_async_remote_copy(
            src_ref=src,
            dst_ref=dst,
            send_sem=send,
            recv_sem=recv,
            device_id={"dp": to},
            device_id_type=pl.DeviceIdType.MESH,
        )

    def chunk(k, q, s):
        return bufs[k].at[pl.ds(pl.multiple_of((4 * q + s) * tokens, tokens), tokens), :]

    def near(k, q):
        return remote(
            bc_ref.at[q, :, k * width : (k + 1) * width],
            chunk(k, quad, spot),
            near_send.at[k, q],
            near_recv.at[k, quad],
            4 * q + spot,
        )

    def near_in(k, q):
        return remote(
            chunk(k, q, spot), chunk(k, q, spot), near_send.at[k, q], near_recv.at[k, q], side
        )

    def to_side(k, q, s):
        return remote(chunk(k, q, s), chunk(k, q, s), side_send.at[k, q], side_recv.at[k, q], side)

    def to_twin(k, q, s):
        return remote(chunk(k, q, s), chunk(k, q, s), twin_send.at[k, q], twin_recv.at[k, q], twin)

    def to_twin_last(k, q, s):
        return remote(chunk(k, q, s), chunk(k, q, s), last_send.at[k, q], last_recv.at[k, q], twin)

    def init_copy(d):
        return remote(s_out.at[d], s_in.at[me], init_send.at[d], init_recv.at[me], d)

    def init_from(d):
        return remote(s_in.at[d], s_in.at[d], init_send.at[d], init_recv.at[d], side)

    def fin_copy(d):
        return remote(f_out.at[d], f_in.at[me], fin_send.at[d], fin_recv.at[me], d)

    def fin_from(d):
        return remote(f_in.at[d], f_in.at[d], fin_send.at[d], fin_recv.at[d], side)

    def every(count, body):
        lax.fori_loop(0, count, lambda i, c: (body(i), c)[1], 0)

    mine = pl.ds(pl.multiple_of(me * tokens, tokens), tokens)
    loads = [
        pltpu.make_async_copy(src, dst, load_sem.at[i])
        for i, (src, dst) in enumerate(
            (
                (st_hbm, st_ref),
                (x_hbm, x_ref),
                (bc_ref.at[quad, :, 0:width], b_buf.at[mine, :]),
                (bc_ref.at[quad, :, width : 2 * width], c_buf.at[mine, :]),
                (z_hbm, z_ref),
            )
        )
    ]
    for load in loads:
        load.start()
    barrier = pltpu.get_barrier_semaphore()

    def greet(i):
        pl.semaphore_signal(
            barrier,
            inc=1,
            device_id={"dp": (me + 1 + i) % devices},
            device_id_type=pl.DeviceIdType.MESH,
        )

    every(devices - 1, greet)

    def narrow(d):
        s_out[d] = st_ref[pl.ds(pl.multiple_of(d * 16, 16), 16), :].astype(jnp.bfloat16)

    loads[0].wait()
    every(devices, narrow)
    pl.semaphore_wait(barrier, devices - 1)

    def send_near(k):
        every(quads - 1, lambda i: near(k, (quad + 1 + i) % quads).start())

    send_near(0)
    every(devices - 1, lambda i: init_copy((me + 1 + i) % devices).start())
    send_near(1)
    s_in[me] = s_out[me]

    wide = dt_ref[...].astype(jnp.float32)
    for j in range(blocks):
        rows_scr[2 * j : 2 * j + 2, :] = wide[:, j * L : (j + 1) * L]
    row = lax.broadcasted_iota(jnp.int32, (2 * blocks, L), 0)
    lane = lax.broadcasted_iota(jnp.int32, (2 * blocks, L), 1)
    first_head = row % 2 == 0
    raw = rows_scr[0 : 2 * blocks, :] + jnp.where(first_head, bias_ref[0], bias_ref[1])
    step = jnp.maximum(raw, 0.0) + jnp.log1p(jnp.exp(-jnp.abs(raw)))
    cum = -step * jnp.where(first_head, rate_ref[0], rate_ref[1])
    shift = 1
    while shift < L:
        cum = cum + jnp.where(lane >= shift, pltpu.roll(cum, shift, 1), 0.0)
        shift *= 2
    total = cum[:, L - 1 : L]
    tail = step * jnp.exp(total - cum)
    growth = jnp.exp(cum)
    rows_scr[0 : 2 * blocks, :] = cum
    rows_scr[2 * blocks : 4 * blocks, :] = step
    edge_scr[...] = jnp.broadcast_to(jnp.exp(total), (2 * blocks, L))
    stacked = jnp.concatenate([cum, tail, growth, step], axis=0)
    cols_scr[...] = jnp.transpose(stacked)

    square_row = lax.broadcasted_iota(jnp.int32, (L, L), 0)
    square_lane = lax.broadcasted_iota(jnp.int32, (L, L), 1)
    causal = square_row >= square_lane
    half = square_lane < L // 2
    gap = 2 * blocks

    def rows_of(j):
        return pl.ds(pl.multiple_of(j * L, L), L)

    def prepare(j):
        turned = pltpu.roll(cols_scr[...], (L - 2 * j) % L, 1)

        def spread(at):
            return jnp.where(half, turned[:, at : at + 1], turned[:, at + 1 : at + 2])

        carried[rows_of(j), :] = (
            x_ref[rows_of(j), :].astype(jnp.float32) * spread(gap)
        ).astype(jnp.bfloat16)
        grow[j] = spread(2 * gap)
        for h in range(2):
            cum_row = rows_scr[pl.ds(2 * j + h, 1), :]
            step_row = rows_scr[pl.ds(gap + 2 * j + h, 1), :]
            log_gap = turned[:, h : h + 1] - cum_row
            pair[2 * j + h] = jnp.exp(jnp.where(causal, log_gap, -jnp.inf)) * step_row

    loads[1].wait()
    every(blocks, prepare)
    loads[2].wait()
    loads[3].wait()
    loads[4].wait()

    def gather(k, work):
        def turn(i):
            @pl.when(i < quads)
            def _():
                q = (quad - i + quads) % quads

                @pl.when(i > 0)
                def _():
                    near_in(k, q).wait_recv()

                to_side(k, q, spot).start()
                to_twin(k, q, spot).start()

            @pl.when((i >= 1) & (i < quads + 1))
            def _():
                q = (quad - i + 1 + quads) % quads
                to_side(k, q, side_spot).wait_recv()
                to_twin_last(k, q, side_spot).start()

            @pl.when(i >= 2)
            def _():
                q = (quad - i + 2 + quads) % quads
                to_twin(k, q, twin_spot).wait_recv()
                to_twin_last(k, q, diag_spot).wait_recv()
                work(2 * q)
                work(2 * q + 1)

        every(quads + 2, turn)

    def add_block(j):
        added[j] = rows_dot(carried[rows_of(j), :], b_buf[rows_of(j), :])

    gather(0, add_block)

    every(devices - 1, lambda i: init_from((me + 1 + i) % devices).wait_recv())
    for k in range(owners):
        for q in range(8):
            piece = s_in[8 * k + q].astype(jnp.float32)
            seeds[k, 8 * q : 8 * q + 8, :] = piece[0:8]
            seeds[k, 64 + 8 * q : 72 + 8 * q, :] = piece[8:16]

    first = [
        sum(
            jnp.where(ps_ref[d] < ps_ref[c], tb_ref[d], 0) for d in range(owners)
        )
        for c in range(owners)
    ]
    end = [first[c] + tb_ref[c] for c in range(owners)]
    state_row = lax.broadcasted_iota(jnp.int32, (L, width), 0)

    def advance(j, state):
        is_start = sum(jnp.where(first[c] == j, 1, 0) for c in range(owners))
        owner = sum(
            jnp.where((first[c] <= j) & (j < end[c]), om_ref[c], 0) for c in range(owners)
        )
        owner = jnp.clip(owner, 0, owners - 1)
        start = jnp.where(is_start > 0, seeds[owner], state)
        starts[j] = start.astype(jnp.bfloat16)
        decay = jnp.where(
            state_row < L // 2,
            edge_scr[pl.ds(2 * j, 1), 0:1],
            edge_scr[pl.ds(2 * j + 1, 1), 0:1],
        )
        after = decay * start + added[j]
        added[j] = after
        return after

    lax.fori_loop(0, blocks, advance, jnp.zeros((L, width), jnp.float32))

    for k in range(owners):
        last = sum(jnp.where(om_ref[c] == k, end[c] - 1, 0) for c in range(owners))
        done = added[jnp.clip(last, 0, blocks - 1)]
        for q in range(8):
            f_out[8 * k + q] = jnp.concatenate(
                [done[8 * q : 8 * q + 8], done[64 + 8 * q : 72 + 8 * q]], axis=0
            ).astype(jnp.bfloat16)
    every(devices - 1, lambda i: fin_copy((me + 1 + i) % devices).start())
    f_in[me] = f_out[me]

    skip_lane = jnp.where(square_lane[0:1] < L // 2, skip_ref[0], skip_ref[1])
    cols_scr[...] = jnp.zeros((L, L), jnp.float32)

    def out_block(j):
        rows = rows_of(j)
        c_block = c_buf[rows, :]
        x_block = x_ref[rows, :]
        scores = lanes_dot(c_block, b_buf[rows, :])
        parts = [
            jnp.dot(
                (scores * pair[2 * j + h]).astype(jnp.bfloat16),
                x_block,
                preferred_element_type=jnp.float32,
            )
            for h in range(2)
        ]
        from_state = grow[j] * lanes_dot(c_block, starts[j])
        mixed = (
            jnp.where(half, parts[0], parts[1])
            + from_state
            + skip_lane * x_block.astype(jnp.float32)
        )
        z_block = z_ref[rows, :].astype(jnp.float32)
        result = mixed * (z_block / (1.0 + jnp.exp(-z_block)))
        gated[rows, :] = result
        total_square = jnp.sum(result * result, axis=1, keepdims=True)
        cols_scr[...] = jnp.where(square_lane == j, total_square, cols_scr[...])

    gather(1, out_block)

    sq_out[...] = jnp.transpose(cols_scr[...])[0:blocks]

    def sq_copy(i):
        other = (spot + 1 + i) % 4
        return remote(sq_out, sq_in.at[spot], sq_send.at[other], sq_recv.at[spot], 4 * quad + other)

    def sq_from(i):
        other = (spot + 1 + i) % 4
        return remote(sq_out, sq_in.at[other], sq_send.at[other], sq_recv.at[other], side)

    every(3, lambda i: sq_copy(i).start())
    sq_in[spot] = sq_out[...]
    every(devices - 1, lambda i: fin_from((me + 1 + i) % devices).wait_recv())

    def widen(d):
        ns_ref[pl.ds(pl.multiple_of(d * 16, 16), 16), :] = f_in[d].astype(jnp.float32)

    every(devices, widen)
    every(3, lambda i: sq_from(i).wait_recv())
    group_square = (sq_in[0] + sq_in[1]) + (sq_in[2] + sq_in[3])
    inverse = lax.rsqrt(group_square / (4 * L) + 1e-05)
    cols_scr[...] = jnp.transpose(
        jnp.concatenate([inverse, jnp.zeros((L - blocks, L), jnp.float32)], axis=0)
    )
    gain = gain_ref[...]

    def norm_block(j):
        turned = pltpu.roll(cols_scr[...], (L - j) % L, 1)
        y_ref[rows_of(j), :] = (gated[rows_of(j), :] * turned[:, 0:1] * gain).astype(jnp.bfloat16)

    every(blocks, norm_block)

    def drain(q):
        for k in range(2):

            @pl.when(q != quad)
            def _():
                near(k, q).wait_send()

            to_side(k, q, spot).wait_send()
            to_twin(k, q, spot).wait_send()
            to_twin_last(k, q, side_spot).wait_send()

    every(quads, drain)

    def drain_states(i):
        d = (me + 1 + i) % devices
        init_copy(d).wait_send()
        fin_copy(d).wait_send()

    every(devices - 1, drain_states)
    every(3, lambda i: sq_copy(i).wait_send())


def fused(
    x_in,
    z_in,
    dt_in,
    bc_in,
    owner_states,
    decay_rate,
    dt_bias,
    skip_d,
    norm_gain,
    owner_map,
    prefill_slot,
    turn_blocks,
):
    devices = lax.axis_size("dp")
    tokens, columns = x_in.shape
    blocks = tokens // BLOCK_LEN
    owners = owner_map.shape[0]
    state = bc_in.shape[2] // 2
    quads = devices // 4
    vmem = pl.BlockSpec(memory_space=pltpu.VMEM)
    smem = pl.BlockSpec(memory_space=pltpu.SMEM)
    f32, bf16 = jnp.float32, jnp.bfloat16
    L = BLOCK_LEN
    dma = pltpu.SemaphoreType.DMA
    y_out, new_states = pl.pallas_call(
        functools.partial(layer_kernel, devices, blocks, owners),
        out_shape=(
            jax.ShapeDtypeStruct((tokens, columns), bf16),
            jax.ShapeDtypeStruct((devices * 16, state), f32),
        ),
        in_specs=[smem] * 6 + [vmem] * 2 + [pl.BlockSpec(memory_space=pl.ANY)] * 4,
        out_specs=(vmem, vmem),
        scratch_shapes=[
            pltpu.VMEM((tokens, columns), bf16),
            pltpu.VMEM((tokens, columns), bf16),
            pltpu.VMEM((devices * 16, state), f32),
            pltpu.VMEM((tokens, state), bf16),
            pltpu.VMEM((tokens, state), bf16),
            pltpu.VMEM((devices, 16, state), bf16),
            pltpu.VMEM((devices, 16, state), bf16),
            pltpu.VMEM((devices, 16, state), bf16),
            pltpu.VMEM((devices, 16, state), bf16),
            pltpu.VMEM((blocks, L), f32),
            pltpu.VMEM((4, blocks, L), f32),
            pltpu.VMEM((owners, L, state), f32),
            pltpu.VMEM((2 * blocks, L, L), f32),
            pltpu.VMEM((blocks, L, L), f32),
            pltpu.VMEM((blocks, L, state), f32),
            pltpu.VMEM((blocks, L, state), bf16),
            pltpu.VMEM((tokens, columns), bf16),
            pltpu.VMEM((tokens, columns), f32),
            pltpu.VMEM((4 * blocks, L), f32),
            pltpu.VMEM((L, L), f32),
            pltpu.VMEM((2 * blocks, L), f32),
        ]
        + [dma((2, quads))] * 8
        + [dma((devices,))] * 4
        + [dma((4,))] * 2
        + [dma((5,))],
        compiler_params=pltpu.CompilerParams(
            collective_id=0, has_side_effects=True, vmem_limit_bytes=40 * 1024 * 1024
        ),
    )(
        owner_map,
        prefill_slot,
        turn_blocks,
        dt_bias,
        decay_rate,
        skip_d,
        dt_in,
        norm_gain.reshape(1, columns),
        x_in,
        z_in,
        bc_in,
        owner_states.reshape(-1, state),
    )
    return (y_out, new_states.reshape(owner_states.shape))


def choose(*arrays):
    x_in, dt_in, bc_in, owner_states, owner_map = (arrays[i] for i in (0, 2, 3, 4, 9))
    devices = lax.axis_size("dp")
    fits = (
        devices == 4 * bc_in.shape[0]
        and x_in.shape[0] == 16 * BLOCK_LEN
        and x_in.shape[1] == BLOCK_LEN
        and dt_in.shape[0] == 2
        and owner_states.shape[1] == 1
        and owner_states.shape[3] == 8
        and devices == 8 * owner_map.shape[0]
    )
    return (fused if fits else shards)(*arrays)


def solution(mesh):
    placed = (
        P("groups", "dp"),
        P("groups", "dp"),
        P("dp", "groups"),
        P(None, ("groups", "dp"), None),
        P(("groups", "dp"), None, None, None, None),
        P("dp"),
        P("dp"),
        P("dp"),
        P("dp"),
        P("groups"),
        P("groups"),
        P("groups"),
    )
    return jax.shard_map(
        choose,
        mesh=mesh,
        in_specs=placed,
        out_specs=(P("groups", "dp"), P(("groups", "dp"), None, None, None, None)),
        check_vma=False,
    )
```

```python
import functools

import jax
import jax.numpy as jnp
from jax import lax
from jax.experimental import pallas as pl
from jax.experimental.pallas import tpu as pltpu
from jax.sharding import PartitionSpec as P

BLOCK_LEN = 128


exact_mode = lax.Precision.HIGHEST


def shortened(x):

    def short(part):
        return part.astype(jnp.bfloat16) if part.dtype == jnp.float32 else part

    return jax.tree.map(short, x)


def from_partner(x, axis, bit):
    return lax.ppermute(x, axis, [(i, i ^ 1 << bit) for i in range(lax.axis_size(axis))])


def packing(prefill_slot, turn_blocks, block_total):
    conv_count = turn_blocks.shape[0]
    conv_ids = jnp.arange(conv_count, dtype=jnp.int32)
    before_mask = (prefill_slot[None, :] < prefill_slot[:, None]).astype(jnp.int32)
    first_block = jnp.sum(before_mask * turn_blocks[None, :], axis=1)
    end_block = first_block + turn_blocks
    block_ids = jnp.arange(block_total, dtype=jnp.int32)
    inside_mask = (block_ids[:, None] >= first_block[None, :]) & (
        block_ids[:, None] < end_block[None, :]
    )
    block_conv = jnp.sum(jnp.where(inside_mask, conv_ids[None, :], 0), axis=1)
    return (first_block, end_block, block_conv)


def fetch_states(owner_states):
    return lax.all_to_all(
        owner_states[0].astype(jnp.bfloat16), "dp", split_axis=1, concat_axis=2, tiled=True
    ).astype(jnp.float32)


def shards(
    x_in,
    z_in,
    dt_in,
    bc_in,
    owner_states,
    decay_rate,
    dt_bias,
    skip_d,
    norm_gain,
    owner_map,
    prefill_slot,
    turn_blocks,
):
    device_count = lax.axis_size("dp")
    token_count = x_in.shape[0]
    head_local = dt_in.shape[0]
    head_width = x_in.shape[1] // head_local
    group_count = bc_in.shape[0]
    state_width = bc_in.shape[2] // 2
    slot_count = owner_states.shape[1]
    channel_part = owner_states.shape[3]
    decode_width = head_width // channel_part
    owner_count = device_count // decode_width
    block_count = token_count // BLOCK_LEN
    conv_count = owner_map.shape[0]
    per_group = device_count // group_count
    first_block, end_block, block_conv = packing(prefill_slot, turn_blocks, block_count)
    slot_of = owner_map % slot_count
    owner_of = owner_map // slot_count
    copies = jnp.repeat(bc_in, per_group, axis=0)
    bc_group = lax.all_to_all(copies, "dp", split_axis=0, concat_axis=1, tiled=True)[0]
    b_part = bc_group[:, :state_width].reshape(block_count, BLOCK_LEN, state_width)
    c_part = bc_group[:, state_width:].reshape(block_count, BLOCK_LEN, state_width)
    c_float = c_part.astype(jnp.float32)
    step_size = jax.nn.softplus(dt_in.astype(jnp.float32) + dt_bias[:, None])
    log_decay = -step_size * decay_rate[:, None]
    cum_decay = jnp.cumsum(log_decay.reshape(head_local, block_count, BLOCK_LEN), axis=2)
    step_blocks = step_size.reshape(head_local, block_count, BLOCK_LEN)
    block_decay = cum_decay[:, :, -1]
    value_blocks = x_in.reshape(block_count, BLOCK_LEN, head_local, head_width)
    gate_blocks = z_in.reshape(block_count, BLOCK_LEN, head_local, head_width)
    scores = jnp.einsum("kts,kus->ktu", c_part, b_part, preferred_element_type=jnp.float32)
    causal = jnp.arange(BLOCK_LEN)[:, None] >= jnp.arange(BLOCK_LEN)[None, :]
    log_gap = cum_decay[:, :, :, None] - cum_decay[:, :, None, :]
    pair_decay = jnp.exp(jnp.where(causal[None, None], log_gap, -jnp.inf))
    weights = (scores[None] * pair_decay * step_blocks[:, :, None, :]).astype(jnp.bfloat16)
    local_out = jnp.einsum(
        "hktu,kuhp->kthp", weights, value_blocks, preferred_element_type=jnp.float32
    )
    tail_scale = jnp.transpose(
        step_blocks * jnp.exp(block_decay[:, :, None] - cum_decay), (1, 2, 0)
    )
    carried = (value_blocks * tail_scale[..., None]).astype(jnp.bfloat16)
    block_input = jnp.einsum("kuhp,kus->khps", carried, b_part, preferred_element_type=jnp.float32)
    block_ids = jnp.arange(block_count, dtype=jnp.int32)
    target_end = jnp.concatenate([block_ids, end_block])
    target_conv = jnp.concatenate([block_conv, jnp.arange(conv_count, dtype=jnp.int32)])
    destination_first = first_block[target_conv]
    link_mask = (block_conv[None, :] == target_conv[:, None]) & (
        block_ids[None, :] < target_end[:, None]
    )
    lead_sum = jnp.concatenate(
        [jnp.zeros((head_local, 1), jnp.float32), jnp.cumsum(block_decay, axis=1)], axis=1
    )
    lead_end = lead_sum[:, target_end]
    carry_weight = jnp.exp(
        jnp.where(link_mask[None], lead_end[:, :, None] - lead_sum[:, None, 1:], -jnp.inf)
    )
    seed_weight = jnp.exp(lead_end - lead_sum[:, destination_first])
    zero_part = jnp.einsum("hrj,jhps->rhps", carry_weight, block_input, precision=exact_mode)
    decay_factor = jnp.transpose(jnp.exp(cum_decay), (1, 2, 0))[..., None]
    shaped = fetch_states(owner_states).reshape(
        slot_count, head_local, owner_count, head_width, state_width
    )
    initial = shaped[slot_of, :, owner_of]
    boundary = zero_part + jnp.transpose(seed_weight)[:, :, None, None] * initial[target_conv]
    state_out = decay_factor * jnp.einsum(
        "kts,khps->kthp", c_float, boundary[:block_count], precision=exact_mode
    )
    final_state = boundary[block_count:]
    mixer_out = local_out + state_out + skip_d[None, None, :, None] * value_blocks
    gated = mixer_out * jax.nn.silu(gate_blocks.astype(jnp.float32))
    gated_rows = gated.reshape(token_count, head_local * head_width)
    part_square = jnp.sum(gated_rows * gated_rows, axis=1)
    group_square = part_square
    for bit_index in range(per_group.bit_length() - 1):
        group_square = group_square + from_partner(shortened(group_square), "dp", bit_index).astype(
            group_square.dtype
        )
    mean_square = group_square / (per_group * head_local * head_width)
    y_out = (gated_rows * lax.rsqrt(mean_square + 1e-05)[:, None] * norm_gain[None, :]).astype(
        jnp.bfloat16
    )
    blank_slots = jnp.zeros(
        (slot_count, head_local, owner_count, head_width, state_width), jnp.float32
    )
    filled = blank_slots.at[slot_of, :, owner_of].set(final_state)
    outgoing = filled.reshape(slot_count, head_local, owner_count * head_width, state_width)
    returned = lax.all_to_all(outgoing, "dp", split_axis=2, concat_axis=1, tiled=True)
    return (y_out, returned[None])


def lanes_dot(a, b):
    return lax.dot_general(a, b, (((1,), (1,)), ((), ())), preferred_element_type=jnp.float32)


def rows_dot(a, b):
    return lax.dot_general(a, b, (((0,), (0,)), ((), ())), preferred_element_type=jnp.float32)


def layer_kernel(
    devices,
    blocks,
    owners,
    om_ref,
    ps_ref,
    tb_ref,
    bias_ref,
    rate_ref,
    skip_ref,
    dt_ref,
    gain_ref,
    x_hbm,
    z_hbm,
    bc_ref,
    st_hbm,
    y_ref,
    ns_ref,
    x_ref,
    z_ref,
    st_ref,
    b_buf,
    c_buf,
    s_out,
    s_in,
    f_out,
    f_in,
    sq_out,
    sq_in,
    seeds,
    pair,
    grow,
    added,
    starts,
    carried,
    gated,
    rows_scr,
    cols_scr,
    edge_scr,
    near_send,
    near_recv,
    side_send,
    side_recv,
    twin_send,
    twin_recv,
    last_send,
    last_recv,
    init_send,
    init_recv,
    fin_send,
    fin_recv,
    sq_send,
    sq_recv,
    load_sem,
):
    me = lax.axis_index("dp")
    L = BLOCK_LEN
    quads = devices // 4
    quad = me // 4
    spot = me % 4
    twin = me + 1 - 2 * (me % 2)
    side = me + 2 - 4 * ((me // 2) % 2)
    twin_spot, side_spot = twin % 4, side % 4
    diag_spot = 3 - spot
    width = b_buf.shape[1]
    bufs = (b_buf, c_buf)
    tokens = bc_ref.shape[1]

    depth_at = quad // 2
    codes = (0 + 4 * 1 + 16 * 2 + 64 * 3, 1 + 4 * 2 + 16 * 0 + 64 * 3, 2 + 4 * 1 + 16 * 3 + 64 * 0, 3 + 4 * 2 + 16 * 1 + 64 * 0)
    code = sum(jnp.where(depth_at == d, codes[d], 0) for d in range(4))

    def nth(i):
        scale = sum(jnp.where(i // 2 == d, 4**d, 0) for d in range(4))
        return 2 * ((code // scale) % 4) + (quad + i) % 2

    def remote(src, dst, send, recv, to):
        return pltpu.make_async_remote_copy(
            src_ref=src,
            dst_ref=dst,
            send_sem=send,
            recv_sem=recv,
            device_id={"dp": to},
            device_id_type=pl.DeviceIdType.MESH,
        )

    def chunk(k, q, s):
        return bufs[k].at[pl.ds(pl.multiple_of((4 * q + s) * tokens, tokens), tokens), :]

    def near(k, q):
        return remote(
            bc_ref.at[q, :, k * width : (k + 1) * width],
            chunk(k, quad, spot),
            near_send.at[k, q],
            near_recv.at[k, quad],
            4 * q + spot,
        )

    def near_in(k, q):
        return remote(
            chunk(k, q, spot), chunk(k, q, spot), near_send.at[k, q], near_recv.at[k, q], side
        )

    def to_side(k, q, s):
        return remote(chunk(k, q, s), chunk(k, q, s), side_send.at[k, q], side_recv.at[k, q], side)

    def to_twin(k, q, s):
        return remote(chunk(k, q, s), chunk(k, q, s), twin_send.at[k, q], twin_recv.at[k, q], twin)

    def to_twin_last(k, q, s):
        return remote(chunk(k, q, s), chunk(k, q, s), last_send.at[k, q], last_recv.at[k, q], twin)

    def init_copy(d):
        return remote(s_out.at[d], s_in.at[me], init_send.at[d], init_recv.at[me], d)

    def init_from(d):
        return remote(s_in.at[d], s_in.at[d], init_send.at[d], init_recv.at[d], side)

    def fin_copy(d):
        return remote(f_out.at[d], f_in.at[me], fin_send.at[d], fin_recv.at[me], d)

    def fin_from(d):
        return remote(f_in.at[d], f_in.at[d], fin_send.at[d], fin_recv.at[d], side)

    def every(count, body):
        lax.fori_loop(0, count, lambda i, c: (body(i), c)[1], 0)

    mine = pl.ds(pl.multiple_of(me * tokens, tokens), tokens)
    loads = [
        pltpu.make_async_copy(src, dst, load_sem.at[i])
        for i, (src, dst) in enumerate(
            (
                (st_hbm, st_ref),
                (x_hbm, x_ref),
                (bc_ref.at[quad, :, 0:width], b_buf.at[mine, :]),
                (bc_ref.at[quad, :, width : 2 * width], c_buf.at[mine, :]),
                (z_hbm, z_ref),
            )
        )
    ]
    for load in loads:
        load.start()
    barrier = pltpu.get_barrier_semaphore()

    def greet(i):
        pl.semaphore_signal(
            barrier,
            inc=1,
            device_id={"dp": (me + 1 + i) % devices},
            device_id_type=pl.DeviceIdType.MESH,
        )

    every(devices - 1, greet)

    def narrow(d):
        s_out[d] = st_ref[pl.ds(pl.multiple_of(d * 16, 16), 16), :].astype(jnp.bfloat16)

    loads[0].wait()
    every(devices, narrow)
    pl.semaphore_wait(barrier, devices - 1)

    every(quads - 1, lambda i: near(0, nth(i + 1)).start())
    every(devices - 1, lambda i: init_copy((me + 1 + i) % devices).start())
    s_in[me] = s_out[me]

    wide = dt_ref[...].astype(jnp.float32)
    for j in range(blocks):
        rows_scr[2 * j : 2 * j + 2, :] = wide[:, j * L : (j + 1) * L]
    row = lax.broadcasted_iota(jnp.int32, (2 * blocks, L), 0)
    lane = lax.broadcasted_iota(jnp.int32, (2 * blocks, L), 1)
    first_head = row % 2 == 0
    raw = rows_scr[0 : 2 * blocks, :] + jnp.where(first_head, bias_ref[0], bias_ref[1])
    step = jnp.maximum(raw, 0.0) + jnp.log1p(jnp.exp(-jnp.abs(raw)))
    cum = -step * jnp.where(first_head, rate_ref[0], rate_ref[1])
    shift = 1
    while shift < L:
        cum = cum + jnp.where(lane >= shift, pltpu.roll(cum, shift, 1), 0.0)
        shift *= 2
    total = cum[:, L - 1 : L]
    tail = step * jnp.exp(total - cum)
    growth = jnp.exp(cum)
    rows_scr[0 : 2 * blocks, :] = cum
    rows_scr[2 * blocks : 4 * blocks, :] = step
    edge_scr[...] = jnp.broadcast_to(jnp.exp(total), (2 * blocks, L))
    stacked = jnp.concatenate([cum, tail, growth, step], axis=0)
    cols_scr[...] = jnp.transpose(stacked)

    square_row = lax.broadcasted_iota(jnp.int32, (L, L), 0)
    square_lane = lax.broadcasted_iota(jnp.int32, (L, L), 1)
    causal = square_row >= square_lane
    half = square_lane < L // 2
    gap = 2 * blocks

    def rows_of(j):
        return pl.ds(pl.multiple_of(j * L, L), L)

    def prepare(j):
        turned = pltpu.roll(cols_scr[...], (L - 2 * j) % L, 1)

        def spread(at):
            return jnp.where(half, turned[:, at : at + 1], turned[:, at + 1 : at + 2])

        carried[rows_of(j), :] = (
            x_ref[rows_of(j), :].astype(jnp.float32) * spread(gap)
        ).astype(jnp.bfloat16)
        grow[j] = spread(2 * gap)
        for h in range(2):
            cum_row = rows_scr[pl.ds(2 * j + h, 1), :]
            step_row = rows_scr[pl.ds(gap + 2 * j + h, 1), :]
            log_gap = turned[:, h : h + 1] - cum_row
            pair[2 * j + h] = jnp.exp(jnp.where(causal, log_gap, -jnp.inf)) * step_row

    loads[1].wait()
    every(blocks, prepare)
    loads[2].wait()
    loads[3].wait()
    loads[4].wait()

    def gather(k, work):
        def turn(i):
            @pl.when(i < quads)
            def _():
                q = nth(i)

                @pl.when(i > 0)
                def _():
                    near_in(k, q).wait_recv()

                to_side(k, q, spot).start()
                to_twin(k, q, spot).start()
                if k == 0:

                    @pl.when(i > 0)
                    def _():
                        near(1, q).start()

            @pl.when((i >= 1) & (i < quads + 1))
            def _():
                q = nth(i - 1)
                to_side(k, q, side_spot).wait_recv()
                to_twin_last(k, q, side_spot).start()

            @pl.when(i >= 2)
            def _():
                q = nth(i - 2)
                to_twin(k, q, twin_spot).wait_recv()
                to_twin_last(k, q, diag_spot).wait_recv()
                work(2 * q)
                work(2 * q + 1)

        every(quads + 2, turn)

    def add_block(j):
        added[j] = rows_dot(carried[rows_of(j), :], b_buf[rows_of(j), :])

    gather(0, add_block)

    every(devices - 1, lambda i: init_from((me + 1 + i) % devices).wait_recv())
    for k in range(owners):
        for q in range(8):
            piece = s_in[8 * k + q].astype(jnp.float32)
            seeds[k, 8 * q : 8 * q + 8, :] = piece[0:8]
            seeds[k, 64 + 8 * q : 72 + 8 * q, :] = piece[8:16]

    first = [
        sum(
            jnp.where(ps_ref[d] < ps_ref[c], tb_ref[d], 0) for d in range(owners)
        )
        for c in range(owners)
    ]
    end = [first[c] + tb_ref[c] for c in range(owners)]
    state_row = lax.broadcasted_iota(jnp.int32, (L, width), 0)

    def advance(j, state):
        is_start = sum(jnp.where(first[c] == j, 1, 0) for c in range(owners))
        owner = sum(
            jnp.where((first[c] <= j) & (j < end[c]), om_ref[c], 0) for c in range(owners)
        )
        owner = jnp.clip(owner, 0, owners - 1)
        start = jnp.where(is_start > 0, seeds[owner], state)
        starts[j] = start.astype(jnp.bfloat16)
        decay = jnp.where(
            state_row < L // 2,
            edge_scr[pl.ds(2 * j, 1), 0:1],
            edge_scr[pl.ds(2 * j + 1, 1), 0:1],
        )
        after = decay * start + added[j]
        added[j] = after
        return after

    lax.fori_loop(0, blocks, advance, jnp.zeros((L, width), jnp.float32))

    for k in range(owners):
        last = sum(jnp.where(om_ref[c] == k, end[c] - 1, 0) for c in range(owners))
        done = added[jnp.clip(last, 0, blocks - 1)]
        for q in range(8):
            f_out[8 * k + q] = jnp.concatenate(
                [done[8 * q : 8 * q + 8], done[64 + 8 * q : 72 + 8 * q]], axis=0
            ).astype(jnp.bfloat16)
    every(devices - 1, lambda i: fin_copy((me + 1 + i) % devices).start())
    f_in[me] = f_out[me]

    skip_lane = jnp.where(square_lane[0:1] < L // 2, skip_ref[0], skip_ref[1])
    cols_scr[...] = jnp.zeros((L, L), jnp.float32)

    def out_block(j):
        rows = rows_of(j)
        c_block = c_buf[rows, :]
        x_block = x_ref[rows, :]
        scores = lanes_dot(c_block, b_buf[rows, :])
        parts = [
            jnp.dot(
                (scores * pair[2 * j + h]).astype(jnp.bfloat16),
                x_block,
                preferred_element_type=jnp.float32,
            )
            for h in range(2)
        ]
        from_state = grow[j] * lanes_dot(c_block, starts[j])
        mixed = (
            jnp.where(half, parts[0], parts[1])
            + from_state
            + skip_lane * x_block.astype(jnp.float32)
        )
        z_block = z_ref[rows, :].astype(jnp.float32)
        result = mixed * (z_block / (1.0 + jnp.exp(-z_block)))
        gated[rows, :] = result
        total_square = jnp.sum(result * result, axis=1, keepdims=True)
        cols_scr[...] = jnp.where(square_lane == j, total_square, cols_scr[...])

    gather(1, out_block)

    sq_out[...] = jnp.transpose(cols_scr[...])[0:blocks]

    def sq_copy(i):
        other = (spot + 1 + i) % 4
        return remote(sq_out, sq_in.at[spot], sq_send.at[other], sq_recv.at[spot], 4 * quad + other)

    def sq_from(i):
        other = (spot + 1 + i) % 4
        return remote(sq_out, sq_in.at[other], sq_send.at[other], sq_recv.at[other], side)

    every(3, lambda i: sq_copy(i).start())
    sq_in[spot] = sq_out[...]
    every(devices - 1, lambda i: fin_from((me + 1 + i) % devices).wait_recv())

    def widen(d):
        ns_ref[pl.ds(pl.multiple_of(d * 16, 16), 16), :] = f_in[d].astype(jnp.float32)

    every(devices, widen)
    every(3, lambda i: sq_from(i).wait_recv())
    group_square = (sq_in[0] + sq_in[1]) + (sq_in[2] + sq_in[3])
    inverse = lax.rsqrt(group_square / (4 * L) + 1e-05)
    cols_scr[...] = jnp.transpose(
        jnp.concatenate([inverse, jnp.zeros((L - blocks, L), jnp.float32)], axis=0)
    )
    gain = gain_ref[...]

    def norm_block(j):
        turned = pltpu.roll(cols_scr[...], (L - j) % L, 1)
        y_ref[rows_of(j), :] = (gated[rows_of(j), :] * turned[:, 0:1] * gain).astype(jnp.bfloat16)

    every(blocks, norm_block)

    def drain(q):
        for k in range(2):

            @pl.when(q != quad)
            def _():
                near(k, q).wait_send()

            to_side(k, q, spot).wait_send()
            to_twin(k, q, spot).wait_send()
            to_twin_last(k, q, side_spot).wait_send()

    every(quads, drain)

    def drain_states(i):
        d = (me + 1 + i) % devices
        init_copy(d).wait_send()
        fin_copy(d).wait_send()

    every(devices - 1, drain_states)
    every(3, lambda i: sq_copy(i).wait_send())


def fused(
    x_in,
    z_in,
    dt_in,
    bc_in,
    owner_states,
    decay_rate,
    dt_bias,
    skip_d,
    norm_gain,
    owner_map,
    prefill_slot,
    turn_blocks,
):
    devices = lax.axis_size("dp")
    tokens, columns = x_in.shape
    blocks = tokens // BLOCK_LEN
    owners = owner_map.shape[0]
    state = bc_in.shape[2] // 2
    quads = devices // 4
    vmem = pl.BlockSpec(memory_space=pltpu.VMEM)
    smem = pl.BlockSpec(memory_space=pltpu.SMEM)
    f32, bf16 = jnp.float32, jnp.bfloat16
    L = BLOCK_LEN
    dma = pltpu.SemaphoreType.DMA
    y_out, new_states = pl.pallas_call(
        functools.partial(layer_kernel, devices, blocks, owners),
        out_shape=(
            jax.ShapeDtypeStruct((tokens, columns), bf16),
            jax.ShapeDtypeStruct((devices * 16, state), f32),
        ),
        in_specs=[smem] * 6 + [vmem] * 2 + [pl.BlockSpec(memory_space=pl.ANY)] * 4,
        out_specs=(vmem, vmem),
        scratch_shapes=[
            pltpu.VMEM((tokens, columns), bf16),
            pltpu.VMEM((tokens, columns), bf16),
            pltpu.VMEM((devices * 16, state), f32),
            pltpu.VMEM((tokens, state), bf16),
            pltpu.VMEM((tokens, state), bf16),
            pltpu.VMEM((devices, 16, state), bf16),
            pltpu.VMEM((devices, 16, state), bf16),
            pltpu.VMEM((devices, 16, state), bf16),
            pltpu.VMEM((devices, 16, state), bf16),
            pltpu.VMEM((blocks, L), f32),
            pltpu.VMEM((4, blocks, L), f32),
            pltpu.VMEM((owners, L, state), f32),
            pltpu.VMEM((2 * blocks, L, L), f32),
            pltpu.VMEM((blocks, L, L), f32),
            pltpu.VMEM((blocks, L, state), f32),
            pltpu.VMEM((blocks, L, state), bf16),
            pltpu.VMEM((tokens, columns), bf16),
            pltpu.VMEM((tokens, columns), f32),
            pltpu.VMEM((4 * blocks, L), f32),
            pltpu.VMEM((L, L), f32),
            pltpu.VMEM((2 * blocks, L), f32),
        ]
        + [dma((2, quads))] * 8
        + [dma((devices,))] * 4
        + [dma((4,))] * 2
        + [dma((5,))],
        compiler_params=pltpu.CompilerParams(
            collective_id=0, has_side_effects=True, vmem_limit_bytes=63 * 1024 * 1024
        ),
    )(
        owner_map,
        prefill_slot,
        turn_blocks,
        dt_bias,
        decay_rate,
        skip_d,
        dt_in,
        norm_gain.reshape(1, columns),
        x_in,
        z_in,
        bc_in,
        owner_states.reshape(-1, state),
    )
    return (y_out, new_states.reshape(owner_states.shape))


def choose(*arrays):
    x_in, dt_in, bc_in, owner_states, owner_map = (arrays[i] for i in (0, 2, 3, 4, 9))
    devices = lax.axis_size("dp")
    fits = (
        devices == 4 * bc_in.shape[0]
        and x_in.shape[0] == 16 * BLOCK_LEN
        and x_in.shape[1] == BLOCK_LEN
        and dt_in.shape[0] == 2
        and owner_states.shape[1] == 1
        and owner_states.shape[3] == 8
        and devices == 8 * owner_map.shape[0]
    )
    return (fused if fits else shards)(*arrays)


def solution(mesh):
    placed = (
        P("groups", "dp"),
        P("groups", "dp"),
        P("dp", "groups"),
        P(None, ("groups", "dp"), None),
        P(("groups", "dp"), None, None, None, None),
        P("dp"),
        P("dp"),
        P("dp"),
        P("dp"),
        P("groups"),
        P("groups"),
        P("groups"),
    )
    return jax.shard_map(
        choose,
        mesh=mesh,
        in_specs=placed,
        out_specs=(P("groups", "dp"), P(("groups", "dp"), None, None, None, None)),
        check_vma=False,
    )
```

```python
import functools

import jax
import jax.numpy as jnp
from jax import lax
from jax.experimental import pallas as pl
from jax.experimental.pallas import tpu as pltpu
from jax.sharding import PartitionSpec as P

BLOCK_LEN = 128


exact_mode = lax.Precision.HIGHEST


def shortened(x):

    def short(part):
        return part.astype(jnp.bfloat16) if part.dtype == jnp.float32 else part

    return jax.tree.map(short, x)


def from_partner(x, axis, bit):
    return lax.ppermute(x, axis, [(i, i ^ 1 << bit) for i in range(lax.axis_size(axis))])


def packing(prefill_slot, turn_blocks, block_total):
    conv_count = turn_blocks.shape[0]
    conv_ids = jnp.arange(conv_count, dtype=jnp.int32)
    before_mask = (prefill_slot[None, :] < prefill_slot[:, None]).astype(jnp.int32)
    first_block = jnp.sum(before_mask * turn_blocks[None, :], axis=1)
    end_block = first_block + turn_blocks
    block_ids = jnp.arange(block_total, dtype=jnp.int32)
    inside_mask = (block_ids[:, None] >= first_block[None, :]) & (
        block_ids[:, None] < end_block[None, :]
    )
    block_conv = jnp.sum(jnp.where(inside_mask, conv_ids[None, :], 0), axis=1)
    return (first_block, end_block, block_conv)


def fetch_states(owner_states):
    return lax.all_to_all(
        owner_states[0].astype(jnp.bfloat16), "dp", split_axis=1, concat_axis=2, tiled=True
    ).astype(jnp.float32)


def shards(
    x_in,
    z_in,
    dt_in,
    bc_in,
    owner_states,
    decay_rate,
    dt_bias,
    skip_d,
    norm_gain,
    owner_map,
    prefill_slot,
    turn_blocks,
):
    device_count = lax.axis_size("dp")
    token_count = x_in.shape[0]
    head_local = dt_in.shape[0]
    head_width = x_in.shape[1] // head_local
    group_count = bc_in.shape[0]
    state_width = bc_in.shape[2] // 2
    slot_count = owner_states.shape[1]
    channel_part = owner_states.shape[3]
    decode_width = head_width // channel_part
    owner_count = device_count // decode_width
    block_count = token_count // BLOCK_LEN
    conv_count = owner_map.shape[0]
    per_group = device_count // group_count
    first_block, end_block, block_conv = packing(prefill_slot, turn_blocks, block_count)
    slot_of = owner_map % slot_count
    owner_of = owner_map // slot_count
    copies = jnp.repeat(bc_in, per_group, axis=0)
    bc_group = lax.all_to_all(copies, "dp", split_axis=0, concat_axis=1, tiled=True)[0]
    b_part = bc_group[:, :state_width].reshape(block_count, BLOCK_LEN, state_width)
    c_part = bc_group[:, state_width:].reshape(block_count, BLOCK_LEN, state_width)
    c_float = c_part.astype(jnp.float32)
    step_size = jax.nn.softplus(dt_in.astype(jnp.float32) + dt_bias[:, None])
    log_decay = -step_size * decay_rate[:, None]
    cum_decay = jnp.cumsum(log_decay.reshape(head_local, block_count, BLOCK_LEN), axis=2)
    step_blocks = step_size.reshape(head_local, block_count, BLOCK_LEN)
    block_decay = cum_decay[:, :, -1]
    value_blocks = x_in.reshape(block_count, BLOCK_LEN, head_local, head_width)
    gate_blocks = z_in.reshape(block_count, BLOCK_LEN, head_local, head_width)
    scores = jnp.einsum("kts,kus->ktu", c_part, b_part, preferred_element_type=jnp.float32)
    causal = jnp.arange(BLOCK_LEN)[:, None] >= jnp.arange(BLOCK_LEN)[None, :]
    log_gap = cum_decay[:, :, :, None] - cum_decay[:, :, None, :]
    pair_decay = jnp.exp(jnp.where(causal[None, None], log_gap, -jnp.inf))
    weights = (scores[None] * pair_decay * step_blocks[:, :, None, :]).astype(jnp.bfloat16)
    local_out = jnp.einsum(
        "hktu,kuhp->kthp", weights, value_blocks, preferred_element_type=jnp.float32
    )
    tail_scale = jnp.transpose(
        step_blocks * jnp.exp(block_decay[:, :, None] - cum_decay), (1, 2, 0)
    )
    carried = (value_blocks * tail_scale[..., None]).astype(jnp.bfloat16)
    block_input = jnp.einsum("kuhp,kus->khps", carried, b_part, preferred_element_type=jnp.float32)
    block_ids = jnp.arange(block_count, dtype=jnp.int32)
    target_end = jnp.concatenate([block_ids, end_block])
    target_conv = jnp.concatenate([block_conv, jnp.arange(conv_count, dtype=jnp.int32)])
    destination_first = first_block[target_conv]
    link_mask = (block_conv[None, :] == target_conv[:, None]) & (
        block_ids[None, :] < target_end[:, None]
    )
    lead_sum = jnp.concatenate(
        [jnp.zeros((head_local, 1), jnp.float32), jnp.cumsum(block_decay, axis=1)], axis=1
    )
    lead_end = lead_sum[:, target_end]
    carry_weight = jnp.exp(
        jnp.where(link_mask[None], lead_end[:, :, None] - lead_sum[:, None, 1:], -jnp.inf)
    )
    seed_weight = jnp.exp(lead_end - lead_sum[:, destination_first])
    zero_part = jnp.einsum("hrj,jhps->rhps", carry_weight, block_input, precision=exact_mode)
    decay_factor = jnp.transpose(jnp.exp(cum_decay), (1, 2, 0))[..., None]
    shaped = fetch_states(owner_states).reshape(
        slot_count, head_local, owner_count, head_width, state_width
    )
    initial = shaped[slot_of, :, owner_of]
    boundary = zero_part + jnp.transpose(seed_weight)[:, :, None, None] * initial[target_conv]
    state_out = decay_factor * jnp.einsum(
        "kts,khps->kthp", c_float, boundary[:block_count], precision=exact_mode
    )
    final_state = boundary[block_count:]
    mixer_out = local_out + state_out + skip_d[None, None, :, None] * value_blocks
    gated = mixer_out * jax.nn.silu(gate_blocks.astype(jnp.float32))
    gated_rows = gated.reshape(token_count, head_local * head_width)
    part_square = jnp.sum(gated_rows * gated_rows, axis=1)
    group_square = part_square
    for bit_index in range(per_group.bit_length() - 1):
        group_square = group_square + from_partner(shortened(group_square), "dp", bit_index).astype(
            group_square.dtype
        )
    mean_square = group_square / (per_group * head_local * head_width)
    y_out = (gated_rows * lax.rsqrt(mean_square + 1e-05)[:, None] * norm_gain[None, :]).astype(
        jnp.bfloat16
    )
    blank_slots = jnp.zeros(
        (slot_count, head_local, owner_count, head_width, state_width), jnp.float32
    )
    filled = blank_slots.at[slot_of, :, owner_of].set(final_state)
    outgoing = filled.reshape(slot_count, head_local, owner_count * head_width, state_width)
    returned = lax.all_to_all(outgoing, "dp", split_axis=2, concat_axis=1, tiled=True)
    return (y_out, returned[None])


def lanes_dot(a, b):
    return lax.dot_general(a, b, (((1,), (1,)), ((), ())), preferred_element_type=jnp.float32)


def rows_dot(a, b):
    return lax.dot_general(a, b, (((0,), (0,)), ((), ())), preferred_element_type=jnp.float32)


def layer_kernel(
    devices,
    blocks,
    owners,
    om_ref,
    ps_ref,
    tb_ref,
    bias_ref,
    rate_ref,
    skip_ref,
    dt_ref,
    gain_ref,
    x_hbm,
    z_hbm,
    bc_ref,
    st_hbm,
    y_ref,
    ns_ref,
    x_ref,
    z_ref,
    st_ref,
    buf,
    s_out,
    s_in,
    f_out,
    f_in,
    sq_out,
    sq_in,
    seeds,
    pair,
    grow,
    added,
    starts,
    carried,
    gated,
    rows_scr,
    cols_scr,
    edge_scr,
    sums_scr,
    near_send,
    near_recv,
    side_send,
    side_recv,
    twin_send,
    twin_recv,
    last_send,
    last_recv,
    init_send,
    init_recv,
    fin_send,
    fin_recv,
    sq_send,
    sq_recv,
    load_sem,
):
    me = lax.axis_index("dp")
    L = BLOCK_LEN
    quads = devices // 4
    quad = me // 4
    spot = me % 4
    twin = me + 1 - 2 * (me % 2)
    side = me + 2 - 4 * ((me // 2) % 2)
    twin_spot, side_spot = twin % 4, side % 4
    diag_spot = 3 - spot
    width = buf.shape[1]
    tokens = bc_ref.shape[1]
    rows_each = devices * tokens

    depth_at = quad // 2
    codes = (0 + 4 * 1 + 16 * 2 + 64 * 3, 1 + 4 * 2 + 16 * 0 + 64 * 3, 2 + 4 * 1 + 16 * 3 + 64 * 0, 3 + 4 * 2 + 16 * 1 + 64 * 0)
    code = sum(jnp.where(depth_at == d, codes[d], 0) for d in range(4))

    def nth(i):
        scale = sum(jnp.where(i // 2 == d, 4**d, 0) for d in range(4))
        return 2 * ((code // scale) % 4) + (quad + i) % 2

    def remote(src, dst, send, recv, to):
        return pltpu.make_async_remote_copy(
            src_ref=src,
            dst_ref=dst,
            send_sem=send,
            recv_sem=recv,
            device_id={"dp": to},
            device_id_type=pl.DeviceIdType.MESH,
        )

    def chunk(k, q, s):
        return buf.at[pl.ds(pl.multiple_of(k * rows_each + (4 * q + s) * tokens, tokens), tokens), :]

    def near(k, q):
        return remote(
            bc_ref.at[q, :, pl.ds(pl.multiple_of(k * width, width), width)],
            chunk(k, quad, spot),
            near_send.at[k, q],
            near_recv.at[k, quad],
            4 * q + spot,
        )

    def near_in(k, q):
        return remote(
            chunk(k, q, spot), chunk(k, q, spot), near_send.at[k, q], near_recv.at[k, q], side
        )

    def to_side(k, q, s):
        return remote(chunk(k, q, s), chunk(k, q, s), side_send.at[k, q], side_recv.at[k, q], side)

    def to_twin(k, q, s):
        return remote(chunk(k, q, s), chunk(k, q, s), twin_send.at[k, q], twin_recv.at[k, q], twin)

    def to_twin_last(k, q, s):
        return remote(chunk(k, q, s), chunk(k, q, s), last_send.at[k, q], last_recv.at[k, q], twin)

    def init_copy(d):
        return remote(s_out.at[d], s_in.at[me], init_send.at[d], init_recv.at[me], d)

    def init_from(d):
        return remote(s_in.at[d], s_in.at[d], init_send.at[d], init_recv.at[d], side)

    def fin_copy(d):
        return remote(f_out.at[d], f_in.at[me], fin_send.at[d], fin_recv.at[me], d)

    def fin_from(d):
        return remote(f_in.at[d], f_in.at[d], fin_send.at[d], fin_recv.at[d], side)

    def every(count, body):
        lax.fori_loop(0, count, lambda i, c: (body(i), c)[1], 0)

    loads = [
        pltpu.make_async_copy(src, dst, load_sem.at[i])
        for i, (src, dst) in enumerate(
            (
                (st_hbm, st_ref),
                (x_hbm, x_ref),
                (bc_ref.at[quad, :, 0:width], chunk(0, quad, spot)),
                (bc_ref.at[quad, :, width : 2 * width], chunk(1, quad, spot)),
                (z_hbm, z_ref),
            )
        )
    ]
    for load in loads:
        load.start()
    barrier = pltpu.get_barrier_semaphore()

    def greet(i):
        pl.semaphore_signal(
            barrier,
            inc=1,
            device_id={"dp": (me + 1 + i) % devices},
            device_id_type=pl.DeviceIdType.MESH,
        )

    every(devices - 1, greet)

    def narrow(d):
        s_out[d] = st_ref[pl.ds(pl.multiple_of(d * 16, 16), 16), :].astype(jnp.bfloat16)

    loads[0].wait()
    every(devices, narrow)
    pl.semaphore_wait(barrier, devices - 1)

    every(quads - 1, lambda i: near(0, nth(i + 1)).start())
    every(devices - 1, lambda i: init_copy((me + 1 + i) % devices).start())
    s_in[me] = s_out[me]

    wide = dt_ref[...].astype(jnp.float32)
    for j in range(blocks):
        rows_scr[2 * j : 2 * j + 2, :] = wide[:, j * L : (j + 1) * L]
    row = lax.broadcasted_iota(jnp.int32, (2 * blocks, L), 0)
    lane = lax.broadcasted_iota(jnp.int32, (2 * blocks, L), 1)
    first_head = row % 2 == 0
    raw = rows_scr[0 : 2 * blocks, :] + jnp.where(first_head, bias_ref[0], bias_ref[1])
    step = jnp.maximum(raw, 0.0) + jnp.log1p(jnp.exp(-jnp.abs(raw)))
    cum = -step * jnp.where(first_head, rate_ref[0], rate_ref[1])
    shift = 1
    while shift < L:
        cum = cum + jnp.where(lane >= shift, pltpu.roll(cum, shift, 1), 0.0)
        shift *= 2
    total = cum[:, L - 1 : L]
    tail = step * jnp.exp(total - cum)
    growth = jnp.exp(cum)
    rows_scr[0 : 2 * blocks, :] = cum
    rows_scr[2 * blocks : 4 * blocks, :] = step
    edge_scr[...] = jnp.broadcast_to(jnp.exp(total), (2 * blocks, L))
    stacked = jnp.concatenate([cum, tail, growth, step], axis=0)
    cols_scr[...] = jnp.transpose(stacked)

    square_row = lax.broadcasted_iota(jnp.int32, (L, L), 0)
    square_lane = lax.broadcasted_iota(jnp.int32, (L, L), 1)
    causal = square_row >= square_lane
    half = square_lane < L // 2
    gap = 2 * blocks

    def rows_of(j):
        return pl.ds(pl.multiple_of(j * L, L), L)

    def prepare(j):
        turned = pltpu.roll(cols_scr[...], (L - 2 * j) % L, 1)

        def spread(at):
            return jnp.where(half, turned[:, at : at + 1], turned[:, at + 1 : at + 2])

        carried[rows_of(j), :] = (
            x_ref[rows_of(j), :].astype(jnp.float32) * spread(gap)
        ).astype(jnp.bfloat16)
        grow[j] = spread(2 * gap)
        for h in range(2):
            cum_row = rows_scr[pl.ds(2 * j + h, 1), :]
            step_row = rows_scr[pl.ds(gap + 2 * j + h, 1), :]
            log_gap = turned[:, h : h + 1] - cum_row
            pair[2 * j + h] = jnp.exp(jnp.where(causal, log_gap, -jnp.inf)) * step_row

    for load in loads[1:]:
        load.wait()

    side_lag, work_lag = 3, 5

    def turn(t):
        @pl.when(t < 2 * quads)
        def _():
            k, i = t // quads, t % quads
            q = nth(i)

            @pl.when(i > 0)
            def _():
                near_in(k, q).wait_recv()

            to_side(k, q, spot).start()
            to_twin(k, q, spot).start()

            @pl.when((t > 0) & (t < quads))
            def _():
                near(1, q).start()

            @pl.when(t < quads)
            def _():
                prepare(2 * q)
                prepare(2 * q + 1)

        @pl.when((t >= side_lag) & (t < 2 * quads + side_lag))
        def _():
            u = t - side_lag
            k, q = u // quads, nth(u % quads)
            to_side(k, q, side_spot).wait_recv()
            to_twin_last(k, q, side_spot).start()

        @pl.when(t >= work_lag)
        def _():
            u = t - work_lag
            k, q = u // quads, nth(u % quads)
            to_twin(k, q, twin_spot).wait_recv()
            to_twin_last(k, q, diag_spot).wait_recv()

            @pl.when(u < quads)
            def _():
                add_block(2 * q)
                add_block(2 * q + 1)

            @pl.when(u >= quads)
            def _():
                out_block(2 * q)
                out_block(2 * q + 1)

    def add_block(j):
        added[j] = rows_dot(carried[rows_of(j), :], buf[rows_of(j), :])

    skip_lane = jnp.where(square_lane[0:1] < L // 2, skip_ref[0], skip_ref[1])

    def out_block(j):
        rows = rows_of(j)
        c_block = buf[pl.ds(pl.multiple_of(rows_each + j * L, L), L), :]
        x_block = x_ref[rows, :]
        scores = lanes_dot(c_block, buf[rows, :])
        parts = [
            jnp.dot(
                (scores * pair[2 * j + h]).astype(jnp.bfloat16),
                x_block,
                preferred_element_type=jnp.float32,
            )
            for h in range(2)
        ]
        from_state = grow[j] * lanes_dot(c_block, starts[j])
        mixed = (
            jnp.where(half, parts[0], parts[1])
            + from_state
            + skip_lane * x_block.astype(jnp.float32)
        )
        z_block = z_ref[rows, :].astype(jnp.float32)
        result = mixed * (z_block / (1.0 + jnp.exp(-z_block)))
        gated[rows, :] = result
        total_square = jnp.sum(result * result, axis=1, keepdims=True)
        sums_scr[...] = jnp.where(square_lane == j, total_square, sums_scr[...])

    every(quads + work_lag, turn)

    every(devices - 1, lambda i: init_from((me + 1 + i) % devices).wait_recv())
    for k in range(owners):
        for q in range(8):
            piece = s_in[8 * k + q].astype(jnp.float32)
            seeds[k, 8 * q : 8 * q + 8, :] = piece[0:8]
            seeds[k, 64 + 8 * q : 72 + 8 * q, :] = piece[8:16]

    first = [
        sum(
            jnp.where(ps_ref[d] < ps_ref[c], tb_ref[d], 0) for d in range(owners)
        )
        for c in range(owners)
    ]
    end = [first[c] + tb_ref[c] for c in range(owners)]
    state_row = lax.broadcasted_iota(jnp.int32, (L, width), 0)

    def advance(j, state):
        is_start = sum(jnp.where(first[c] == j, 1, 0) for c in range(owners))
        owner = sum(
            jnp.where((first[c] <= j) & (j < end[c]), om_ref[c], 0) for c in range(owners)
        )
        owner = jnp.clip(owner, 0, owners - 1)
        start = jnp.where(is_start > 0, seeds[owner], state)
        starts[j] = start.astype(jnp.bfloat16)
        decay = jnp.where(
            state_row < L // 2,
            edge_scr[pl.ds(2 * j, 1), 0:1],
            edge_scr[pl.ds(2 * j + 1, 1), 0:1],
        )
        after = decay * start + added[j]
        added[j] = after
        return after

    lax.fori_loop(0, blocks, advance, jnp.zeros((L, width), jnp.float32))

    for k in range(owners):
        last = sum(jnp.where(om_ref[c] == k, end[c] - 1, 0) for c in range(owners))
        done = added[jnp.clip(last, 0, blocks - 1)]
        for q in range(8):
            f_out[8 * k + q] = jnp.concatenate(
                [done[8 * q : 8 * q + 8], done[64 + 8 * q : 72 + 8 * q]], axis=0
            ).astype(jnp.bfloat16)
    every(devices - 1, lambda i: fin_copy((me + 1 + i) % devices).start())
    f_in[me] = f_out[me]

    sums_scr[...] = jnp.zeros((L, L), jnp.float32)

    lax.fori_loop(quads + work_lag, 2 * quads + work_lag, lambda t, c: (turn(t), c)[1], 0)

    sq_out[...] = jnp.transpose(sums_scr[...])[0:blocks]

    def sq_copy(i):
        other = (spot + 1 + i) % 4
        return remote(sq_out, sq_in.at[spot], sq_send.at[other], sq_recv.at[spot], 4 * quad + other)

    def sq_from(i):
        other = (spot + 1 + i) % 4
        return remote(sq_out, sq_in.at[other], sq_send.at[other], sq_recv.at[other], side)

    every(3, lambda i: sq_copy(i).start())
    sq_in[spot] = sq_out[...]
    every(devices - 1, lambda i: fin_from((me + 1 + i) % devices).wait_recv())

    def widen(d):
        ns_ref[pl.ds(pl.multiple_of(d * 16, 16), 16), :] = f_in[d]

    every(devices, widen)
    every(3, lambda i: sq_from(i).wait_recv())
    group_square = (sq_in[0] + sq_in[1]) + (sq_in[2] + sq_in[3])
    inverse = lax.rsqrt(group_square / (4 * L) + 1e-05)
    cols_scr[...] = jnp.transpose(
        jnp.concatenate([inverse, jnp.zeros((L - blocks, L), jnp.float32)], axis=0)
    )
    gain = gain_ref[...]

    def norm_block(j):
        turned = pltpu.roll(cols_scr[...], (L - j) % L, 1)
        y_ref[rows_of(j), :] = (gated[rows_of(j), :] * turned[:, 0:1] * gain).astype(jnp.bfloat16)

    every(blocks, norm_block)

    def drain(q):
        for k in range(2):

            @pl.when(q != quad)
            def _():
                near(k, q).wait_send()

            to_side(k, q, spot).wait_send()
            to_twin(k, q, spot).wait_send()
            to_twin_last(k, q, side_spot).wait_send()

    every(quads, drain)

    def drain_states(i):
        d = (me + 1 + i) % devices
        init_copy(d).wait_send()
        fin_copy(d).wait_send()

    every(devices - 1, drain_states)
    every(3, lambda i: sq_copy(i).wait_send())


def fused(
    x_in,
    z_in,
    dt_in,
    bc_in,
    owner_states,
    decay_rate,
    dt_bias,
    skip_d,
    norm_gain,
    owner_map,
    prefill_slot,
    turn_blocks,
):
    devices = lax.axis_size("dp")
    tokens, columns = x_in.shape
    blocks = tokens // BLOCK_LEN
    owners = owner_map.shape[0]
    state = bc_in.shape[2] // 2
    quads = devices // 4
    vmem = pl.BlockSpec(memory_space=pltpu.VMEM)
    smem = pl.BlockSpec(memory_space=pltpu.SMEM)
    f32, bf16 = jnp.float32, jnp.bfloat16
    L = BLOCK_LEN
    dma = pltpu.SemaphoreType.DMA
    y_out, new_states = pl.pallas_call(
        functools.partial(layer_kernel, devices, blocks, owners),
        out_shape=(
            jax.ShapeDtypeStruct((tokens, columns), bf16),
            jax.ShapeDtypeStruct((devices * 16, state), bf16),
        ),
        in_specs=[smem] * 6 + [vmem] * 2 + [pl.BlockSpec(memory_space=pl.ANY)] * 4,
        out_specs=(vmem, vmem),
        scratch_shapes=[
            pltpu.VMEM((tokens, columns), bf16),
            pltpu.VMEM((tokens, columns), bf16),
            pltpu.VMEM((devices * 16, state), f32),
            pltpu.VMEM((2 * tokens, state), bf16),
            pltpu.VMEM((devices, 16, state), bf16),
            pltpu.VMEM((devices, 16, state), bf16),
            pltpu.VMEM((devices, 16, state), bf16),
            pltpu.VMEM((devices, 16, state), bf16),
            pltpu.VMEM((blocks, L), f32),
            pltpu.VMEM((4, blocks, L), f32),
            pltpu.VMEM((owners, L, state), f32),
            pltpu.VMEM((2 * blocks, L, L), f32),
            pltpu.VMEM((blocks, L, L), f32),
            pltpu.VMEM((blocks, L, state), f32),
            pltpu.VMEM((blocks, L, state), bf16),
            pltpu.VMEM((tokens, columns), bf16),
            pltpu.VMEM((tokens, columns), f32),
            pltpu.VMEM((4 * blocks, L), f32),
            pltpu.VMEM((L, L), f32),
            pltpu.VMEM((2 * blocks, L), f32),
            pltpu.VMEM((L, L), f32),
        ]
        + [dma((2, quads))] * 8
        + [dma((devices,))] * 4
        + [dma((4,))] * 2
        + [dma((5,))],
        compiler_params=pltpu.CompilerParams(
            collective_id=0, has_side_effects=True, vmem_limit_bytes=63 * 1024 * 1024
        ),
    )(
        owner_map,
        prefill_slot,
        turn_blocks,
        dt_bias,
        decay_rate,
        skip_d,
        dt_in,
        norm_gain.reshape(1, columns),
        x_in,
        z_in,
        bc_in,
        owner_states.reshape(-1, state),
    )
    return (y_out, new_states.astype(f32).reshape(owner_states.shape))


def choose(*arrays):
    x_in, dt_in, bc_in, owner_states, owner_map = (arrays[i] for i in (0, 2, 3, 4, 9))
    devices = lax.axis_size("dp")
    fits = (
        devices == 4 * bc_in.shape[0]
        and x_in.shape[0] == 16 * BLOCK_LEN
        and x_in.shape[1] == BLOCK_LEN
        and dt_in.shape[0] == 2
        and owner_states.shape[1] == 1
        and owner_states.shape[3] == 8
        and devices == 8 * owner_map.shape[0]
    )
    return (fused if fits else shards)(*arrays)


def solution(mesh):
    placed = (
        P("groups", "dp"),
        P("groups", "dp"),
        P("dp", "groups"),
        P(None, ("groups", "dp"), None),
        P(("groups", "dp"), None, None, None, None),
        P("dp"),
        P("dp"),
        P("dp"),
        P("dp"),
        P("groups"),
        P("groups"),
        P("groups"),
    )
    return jax.shard_map(
        choose,
        mesh=mesh,
        in_specs=placed,
        out_specs=(P("groups", "dp"), P(("groups", "dp"), None, None, None, None)),
        check_vma=False,
    )
```

```python
import functools

import jax
import jax.numpy as jnp
from jax import lax
from jax.experimental import pallas as pl
from jax.experimental.pallas import tpu as pltpu
from jax.sharding import PartitionSpec as P

BLOCK_LEN = 128


exact_mode = lax.Precision.HIGHEST


def shortened(x):

    def short(part):
        return part.astype(jnp.bfloat16) if part.dtype == jnp.float32 else part

    return jax.tree.map(short, x)


def from_partner(x, axis, bit):
    return lax.ppermute(x, axis, [(i, i ^ 1 << bit) for i in range(lax.axis_size(axis))])


def packing(prefill_slot, turn_blocks, block_total):
    conv_count = turn_blocks.shape[0]
    conv_ids = jnp.arange(conv_count, dtype=jnp.int32)
    before_mask = (prefill_slot[None, :] < prefill_slot[:, None]).astype(jnp.int32)
    first_block = jnp.sum(before_mask * turn_blocks[None, :], axis=1)
    end_block = first_block + turn_blocks
    block_ids = jnp.arange(block_total, dtype=jnp.int32)
    inside_mask = (block_ids[:, None] >= first_block[None, :]) & (
        block_ids[:, None] < end_block[None, :]
    )
    block_conv = jnp.sum(jnp.where(inside_mask, conv_ids[None, :], 0), axis=1)
    return (first_block, end_block, block_conv)


def fetch_states(owner_states):
    return lax.all_to_all(
        owner_states[0].astype(jnp.bfloat16), "dp", split_axis=1, concat_axis=2, tiled=True
    ).astype(jnp.float32)


def shards(
    x_in,
    z_in,
    dt_in,
    bc_in,
    owner_states,
    decay_rate,
    dt_bias,
    skip_d,
    norm_gain,
    owner_map,
    prefill_slot,
    turn_blocks,
):
    device_count = lax.axis_size("dp")
    token_count = x_in.shape[0]
    head_local = dt_in.shape[0]
    head_width = x_in.shape[1] // head_local
    group_count = bc_in.shape[0]
    state_width = bc_in.shape[2] // 2
    slot_count = owner_states.shape[1]
    channel_part = owner_states.shape[3]
    decode_width = head_width // channel_part
    owner_count = device_count // decode_width
    block_count = token_count // BLOCK_LEN
    conv_count = owner_map.shape[0]
    per_group = device_count // group_count
    first_block, end_block, block_conv = packing(prefill_slot, turn_blocks, block_count)
    slot_of = owner_map % slot_count
    owner_of = owner_map // slot_count
    copies = jnp.repeat(bc_in, per_group, axis=0)
    bc_group = lax.all_to_all(copies, "dp", split_axis=0, concat_axis=1, tiled=True)[0]
    b_part = bc_group[:, :state_width].reshape(block_count, BLOCK_LEN, state_width)
    c_part = bc_group[:, state_width:].reshape(block_count, BLOCK_LEN, state_width)
    c_float = c_part.astype(jnp.float32)
    step_size = jax.nn.softplus(dt_in.astype(jnp.float32) + dt_bias[:, None])
    log_decay = -step_size * decay_rate[:, None]
    cum_decay = jnp.cumsum(log_decay.reshape(head_local, block_count, BLOCK_LEN), axis=2)
    step_blocks = step_size.reshape(head_local, block_count, BLOCK_LEN)
    block_decay = cum_decay[:, :, -1]
    value_blocks = x_in.reshape(block_count, BLOCK_LEN, head_local, head_width)
    gate_blocks = z_in.reshape(block_count, BLOCK_LEN, head_local, head_width)
    scores = jnp.einsum("kts,kus->ktu", c_part, b_part, preferred_element_type=jnp.float32)
    causal = jnp.arange(BLOCK_LEN)[:, None] >= jnp.arange(BLOCK_LEN)[None, :]
    log_gap = cum_decay[:, :, :, None] - cum_decay[:, :, None, :]
    pair_decay = jnp.exp(jnp.where(causal[None, None], log_gap, -jnp.inf))
    weights = (scores[None] * pair_decay * step_blocks[:, :, None, :]).astype(jnp.bfloat16)
    local_out = jnp.einsum(
        "hktu,kuhp->kthp", weights, value_blocks, preferred_element_type=jnp.float32
    )
    tail_scale = jnp.transpose(
        step_blocks * jnp.exp(block_decay[:, :, None] - cum_decay), (1, 2, 0)
    )
    carried = (value_blocks * tail_scale[..., None]).astype(jnp.bfloat16)
    block_input = jnp.einsum("kuhp,kus->khps", carried, b_part, preferred_element_type=jnp.float32)
    block_ids = jnp.arange(block_count, dtype=jnp.int32)
    target_end = jnp.concatenate([block_ids, end_block])
    target_conv = jnp.concatenate([block_conv, jnp.arange(conv_count, dtype=jnp.int32)])
    destination_first = first_block[target_conv]
    link_mask = (block_conv[None, :] == target_conv[:, None]) & (
        block_ids[None, :] < target_end[:, None]
    )
    lead_sum = jnp.concatenate(
        [jnp.zeros((head_local, 1), jnp.float32), jnp.cumsum(block_decay, axis=1)], axis=1
    )
    lead_end = lead_sum[:, target_end]
    carry_weight = jnp.exp(
        jnp.where(link_mask[None], lead_end[:, :, None] - lead_sum[:, None, 1:], -jnp.inf)
    )
    seed_weight = jnp.exp(lead_end - lead_sum[:, destination_first])
    zero_part = jnp.einsum("hrj,jhps->rhps", carry_weight, block_input, precision=exact_mode)
    decay_factor = jnp.transpose(jnp.exp(cum_decay), (1, 2, 0))[..., None]
    shaped = fetch_states(owner_states).reshape(
        slot_count, head_local, owner_count, head_width, state_width
    )
    initial = shaped[slot_of, :, owner_of]
    boundary = zero_part + jnp.transpose(seed_weight)[:, :, None, None] * initial[target_conv]
    state_out = decay_factor * jnp.einsum(
        "kts,khps->kthp", c_float, boundary[:block_count], precision=exact_mode
    )
    final_state = boundary[block_count:]
    mixer_out = local_out + state_out + skip_d[None, None, :, None] * value_blocks
    gated = mixer_out * jax.nn.silu(gate_blocks.astype(jnp.float32))
    gated_rows = gated.reshape(token_count, head_local * head_width)
    part_square = jnp.sum(gated_rows * gated_rows, axis=1)
    group_square = part_square
    for bit_index in range(per_group.bit_length() - 1):
        group_square = group_square + from_partner(shortened(group_square), "dp", bit_index).astype(
            group_square.dtype
        )
    mean_square = group_square / (per_group * head_local * head_width)
    y_out = (gated_rows * lax.rsqrt(mean_square + 1e-05)[:, None] * norm_gain[None, :]).astype(
        jnp.bfloat16
    )
    blank_slots = jnp.zeros(
        (slot_count, head_local, owner_count, head_width, state_width), jnp.float32
    )
    filled = blank_slots.at[slot_of, :, owner_of].set(final_state)
    outgoing = filled.reshape(slot_count, head_local, owner_count * head_width, state_width)
    returned = lax.all_to_all(outgoing, "dp", split_axis=2, concat_axis=1, tiled=True)
    return (y_out, returned[None])


def lanes_dot(a, b):
    return lax.dot_general(a, b, (((1,), (1,)), ((), ())), preferred_element_type=jnp.float32)


def rows_dot(a, b):
    return lax.dot_general(a, b, (((0,), (0,)), ((), ())), preferred_element_type=jnp.float32)


def layer_kernel(
    devices,
    blocks,
    owners,
    om_ref,
    ps_ref,
    tb_ref,
    bias_ref,
    rate_ref,
    skip_ref,
    dt_ref,
    gain_ref,
    x_hbm,
    z_hbm,
    bc_ref,
    st_hbm,
    y_ref,
    ns_ref,
    x_ref,
    z_ref,
    st_ref,
    buf,
    s_out,
    s_in,
    f_out,
    f_in,
    sq_out,
    sq_in,
    seeds,
    pair,
    grow,
    added,
    starts,
    carried,
    gated,
    rows_scr,
    cols_scr,
    edge_scr,
    sums_scr,
    near_send,
    near_recv,
    side_send,
    side_recv,
    twin_send,
    twin_recv,
    last_send,
    last_recv,
    init_send,
    init_recv,
    fin_send,
    fin_recv,
    sq_send,
    sq_recv,
    load_sem,
):
    me = lax.axis_index("dp")
    L = BLOCK_LEN
    quads = devices // 4
    quad = me // 4
    spot = me % 4
    twin = me + 1 - 2 * (me % 2)
    side = me + 2 - 4 * ((me // 2) % 2)
    twin_spot, side_spot = twin % 4, side % 4
    diag_spot = 3 - spot
    width = buf.shape[1]
    tokens = bc_ref.shape[1]
    rows_each = devices * tokens

    depth_at = quad // 2
    codes = (0 + 4 * 1 + 16 * 2 + 64 * 3, 1 + 4 * 2 + 16 * 0 + 64 * 3, 2 + 4 * 1 + 16 * 3 + 64 * 0, 3 + 4 * 2 + 16 * 1 + 64 * 0)
    code = sum(jnp.where(depth_at == d, codes[d], 0) for d in range(4))

    def nth(i):
        scale = sum(jnp.where(i // 2 == d, 4**d, 0) for d in range(4))
        return 2 * ((code // scale) % 4) + (quad + i) % 2

    def remote(src, dst, send, recv, to):
        return pltpu.make_async_remote_copy(
            src_ref=src,
            dst_ref=dst,
            send_sem=send,
            recv_sem=recv,
            device_id={"dp": to},
            device_id_type=pl.DeviceIdType.MESH,
        )

    def chunk(k, q, s):
        return buf.at[pl.ds(pl.multiple_of(k * rows_each + (4 * q + s) * tokens, tokens), tokens), :]

    def near(k, q):
        return remote(
            bc_ref.at[q, :, pl.ds(pl.multiple_of(k * width, width), width)],
            chunk(k, quad, spot),
            near_send.at[k, q],
            near_recv.at[k, quad],
            4 * q + spot,
        )

    def near_in(k, q):
        return remote(
            chunk(k, q, spot), chunk(k, q, spot), near_send.at[k, q], near_recv.at[k, q], side
        )

    def to_side(k, q, s):
        return remote(chunk(k, q, s), chunk(k, q, s), side_send.at[k, q], side_recv.at[k, q], side)

    def to_twin(k, q, s):
        return remote(chunk(k, q, s), chunk(k, q, s), twin_send.at[k, q], twin_recv.at[k, q], twin)

    def to_twin_last(k, q, s):
        return remote(chunk(k, q, s), chunk(k, q, s), last_send.at[k, q], last_recv.at[k, q], twin)

    def init_copy(d):
        return remote(s_out.at[d], s_in.at[me], init_send.at[d], init_recv.at[me], d)

    def init_from(d):
        return remote(s_in.at[d], s_in.at[d], init_send.at[d], init_recv.at[d], side)

    def fin_copy(d):
        return remote(f_out.at[d], f_in.at[me], fin_send.at[d], fin_recv.at[me], d)

    def fin_from(d):
        return remote(f_in.at[d], f_in.at[d], fin_send.at[d], fin_recv.at[d], side)

    def every(count, body):
        lax.fori_loop(0, count, lambda i, c: (body(i), c)[1], 0)

    loads = [
        pltpu.make_async_copy(src, dst, load_sem.at[i])
        for i, (src, dst) in enumerate(
            (
                (st_hbm, st_ref),
                (x_hbm, x_ref),
                (bc_ref.at[quad, :, 0:width], chunk(0, quad, spot)),
                (bc_ref.at[quad, :, width : 2 * width], chunk(1, quad, spot)),
                (z_hbm, z_ref),
            )
        )
    ]
    for load in loads:
        load.start()
    barrier = pltpu.get_barrier_semaphore()

    def greet(i):
        pl.semaphore_signal(
            barrier,
            inc=1,
            device_id={"dp": (me + 1 + i) % devices},
            device_id_type=pl.DeviceIdType.MESH,
        )

    every(devices - 1, greet)

    def narrow(d):
        s_out[d] = st_ref[pl.ds(pl.multiple_of(d * 16, 16), 16), :].astype(jnp.bfloat16)

    loads[0].wait()
    every(devices, narrow)
    pl.semaphore_wait(barrier, devices - 1)

    every(quads - 1, lambda i: near(0, nth(i + 1)).start())
    every(devices - 1, lambda i: init_copy((me + 1 + i) % devices).start())
    s_in[me] = s_out[me]

    wide = dt_ref[...].astype(jnp.float32)
    for j in range(blocks):
        rows_scr[2 * j : 2 * j + 2, :] = wide[:, j * L : (j + 1) * L]
    row = lax.broadcasted_iota(jnp.int32, (2 * blocks, L), 0)
    lane = lax.broadcasted_iota(jnp.int32, (2 * blocks, L), 1)
    first_head = row % 2 == 0
    raw = rows_scr[0 : 2 * blocks, :] + jnp.where(first_head, bias_ref[0], bias_ref[1])
    step = jnp.maximum(raw, 0.0) + jnp.log1p(jnp.exp(-jnp.abs(raw)))
    cum = -step * jnp.where(first_head, rate_ref[0], rate_ref[1])
    shift = 1
    while shift < L:
        cum = cum + jnp.where(lane >= shift, pltpu.roll(cum, shift, 1), 0.0)
        shift *= 2
    total = cum[:, L - 1 : L]
    tail = step * jnp.exp(total - cum)
    growth = jnp.exp(cum)
    rows_scr[0 : 2 * blocks, :] = cum
    rows_scr[2 * blocks : 4 * blocks, :] = step
    edge_scr[...] = jnp.broadcast_to(jnp.exp(total), (2 * blocks, L))
    stacked = jnp.concatenate([cum, tail, growth, step], axis=0)
    cols_scr[...] = jnp.transpose(stacked)

    square_row = lax.broadcasted_iota(jnp.int32, (L, L), 0)
    square_lane = lax.broadcasted_iota(jnp.int32, (L, L), 1)
    causal = square_row >= square_lane
    half = square_lane < L // 2
    gap = 2 * blocks

    def rows_of(j):
        return pl.ds(pl.multiple_of(j * L, L), L)

    def prepare(j):
        turned = pltpu.roll(cols_scr[...], (L - 2 * j) % L, 1)

        def spread(at):
            return jnp.where(half, turned[:, at : at + 1], turned[:, at + 1 : at + 2])

        carried[rows_of(j), :] = (
            x_ref[rows_of(j), :].astype(jnp.float32) * spread(gap)
        ).astype(jnp.bfloat16)
        grow[j] = spread(2 * gap)
        for h in range(2):
            cum_row = rows_scr[pl.ds(2 * j + h, 1), :]
            step_row = rows_scr[pl.ds(gap + 2 * j + h, 1), :]
            log_gap = turned[:, h : h + 1] - cum_row
            pair[2 * j + h] = jnp.exp(jnp.where(causal, log_gap, -jnp.inf)) * step_row

    for load in loads[1:]:
        load.wait()

    side_lag, work_lag = 5, 8

    def turn(t):
        @pl.when(t < 2 * quads)
        def _():
            k, i = t // quads, t % quads
            q = nth(i)

            @pl.when(i > 0)
            def _():
                near_in(k, q).wait_recv()

            to_side(k, q, spot).start()
            to_twin(k, q, spot).start()

            @pl.when((t > 0) & (t < quads))
            def _():
                near(1, q).start()

            @pl.when(t < quads)
            def _():
                prepare(2 * q)
                prepare(2 * q + 1)

        @pl.when((t >= side_lag) & (t < 2 * quads + side_lag))
        def _():
            u = t - side_lag
            k, q = u // quads, nth(u % quads)
            to_side(k, q, side_spot).wait_recv()
            to_twin_last(k, q, side_spot).start()

        @pl.when(t >= work_lag)
        def _():
            u = t - work_lag
            k, q = u // quads, nth(u % quads)
            to_twin(k, q, twin_spot).wait_recv()
            to_twin_last(k, q, diag_spot).wait_recv()

            @pl.when(u < quads)
            def _():
                add_block(2 * q)
                add_block(2 * q + 1)

            @pl.when(u >= quads)
            def _():
                out_block(2 * q)
                out_block(2 * q + 1)

    def add_block(j):
        added[j] = rows_dot(carried[rows_of(j), :], buf[rows_of(j), :])

    skip_lane = jnp.where(square_lane[0:1] < L // 2, skip_ref[0], skip_ref[1])

    def out_block(j):
        rows = rows_of(j)
        c_block = buf[pl.ds(pl.multiple_of(rows_each + j * L, L), L), :]
        x_block = x_ref[rows, :]
        scores = lanes_dot(c_block, buf[rows, :])
        parts = [
            jnp.dot(
                (scores * pair[2 * j + h]).astype(jnp.bfloat16),
                x_block,
                preferred_element_type=jnp.float32,
            )
            for h in range(2)
        ]
        from_state = grow[j] * lanes_dot(c_block, starts[j])
        mixed = (
            jnp.where(half, parts[0], parts[1])
            + from_state
            + skip_lane * x_block.astype(jnp.float32)
        )
        z_block = z_ref[rows, :].astype(jnp.float32)
        result = mixed * (z_block / (1.0 + jnp.exp(-z_block)))
        gated[rows, :] = result
        total_square = jnp.sum(result * result, axis=1, keepdims=True)
        sums_scr[...] = jnp.where(square_lane == j, total_square, sums_scr[...])

    every(quads + work_lag, turn)

    every(devices - 1, lambda i: init_from((me + 1 + i) % devices).wait_recv())
    for k in range(owners):
        for q in range(8):
            piece = s_in[8 * k + q].astype(jnp.float32)
            seeds[k, 8 * q : 8 * q + 8, :] = piece[0:8]
            seeds[k, 64 + 8 * q : 72 + 8 * q, :] = piece[8:16]

    first = [
        sum(
            jnp.where(ps_ref[d] < ps_ref[c], tb_ref[d], 0) for d in range(owners)
        )
        for c in range(owners)
    ]
    end = [first[c] + tb_ref[c] for c in range(owners)]
    state_row = lax.broadcasted_iota(jnp.int32, (L, width), 0)

    def advance(j, state):
        is_start = sum(jnp.where(first[c] == j, 1, 0) for c in range(owners))
        owner = sum(
            jnp.where((first[c] <= j) & (j < end[c]), om_ref[c], 0) for c in range(owners)
        )
        owner = jnp.clip(owner, 0, owners - 1)
        start = jnp.where(is_start > 0, seeds[owner], state)
        starts[j] = start.astype(jnp.bfloat16)
        decay = jnp.where(
            state_row < L // 2,
            edge_scr[pl.ds(2 * j, 1), 0:1],
            edge_scr[pl.ds(2 * j + 1, 1), 0:1],
        )
        after = decay * start + added[j]
        added[j] = after
        return after

    lax.fori_loop(0, blocks, advance, jnp.zeros((L, width), jnp.float32))

    for k in range(owners):
        last = sum(jnp.where(om_ref[c] == k, end[c] - 1, 0) for c in range(owners))
        done = added[jnp.clip(last, 0, blocks - 1)]
        for q in range(8):
            f_out[8 * k + q] = jnp.concatenate(
                [done[8 * q : 8 * q + 8], done[64 + 8 * q : 72 + 8 * q]], axis=0
            ).astype(jnp.bfloat16)
    every(devices - 1, lambda i: fin_copy((me + 1 + i) % devices).start())
    f_in[me] = f_out[me]

    sums_scr[...] = jnp.zeros((L, L), jnp.float32)

    lax.fori_loop(quads + work_lag, 2 * quads + work_lag, lambda t, c: (turn(t), c)[1], 0)

    sq_out[...] = jnp.transpose(sums_scr[...])[0:blocks]

    def sq_copy(i):
        other = (spot + 1 + i) % 4
        return remote(sq_out, sq_in.at[spot], sq_send.at[other], sq_recv.at[spot], 4 * quad + other)

    def sq_from(i):
        other = (spot + 1 + i) % 4
        return remote(sq_out, sq_in.at[other], sq_send.at[other], sq_recv.at[other], side)

    every(3, lambda i: sq_copy(i).start())
    sq_in[spot] = sq_out[...]
    every(devices - 1, lambda i: fin_from((me + 1 + i) % devices).wait_recv())

    def widen(d):
        ns_ref[pl.ds(pl.multiple_of(d * 16, 16), 16), :] = f_in[d]

    every(devices, widen)
    every(3, lambda i: sq_from(i).wait_recv())
    group_square = (sq_in[0] + sq_in[1]) + (sq_in[2] + sq_in[3])
    inverse = lax.rsqrt(group_square / (4 * L) + 1e-05)
    cols_scr[...] = jnp.transpose(
        jnp.concatenate([inverse, jnp.zeros((L - blocks, L), jnp.float32)], axis=0)
    )
    gain = gain_ref[...]

    def norm_block(j):
        turned = pltpu.roll(cols_scr[...], (L - j) % L, 1)
        y_ref[rows_of(j), :] = (gated[rows_of(j), :] * turned[:, 0:1] * gain).astype(jnp.bfloat16)

    every(blocks, norm_block)

    def drain(q):
        for k in range(2):

            @pl.when(q != quad)
            def _():
                near(k, q).wait_send()

            to_side(k, q, spot).wait_send()
            to_twin(k, q, spot).wait_send()
            to_twin_last(k, q, side_spot).wait_send()

    every(quads, drain)

    def drain_states(i):
        d = (me + 1 + i) % devices
        init_copy(d).wait_send()
        fin_copy(d).wait_send()

    every(devices - 1, drain_states)
    every(3, lambda i: sq_copy(i).wait_send())


def fused(
    x_in,
    z_in,
    dt_in,
    bc_in,
    owner_states,
    decay_rate,
    dt_bias,
    skip_d,
    norm_gain,
    owner_map,
    prefill_slot,
    turn_blocks,
):
    devices = lax.axis_size("dp")
    tokens, columns = x_in.shape
    blocks = tokens // BLOCK_LEN
    owners = owner_map.shape[0]
    state = bc_in.shape[2] // 2
    quads = devices // 4
    vmem = pl.BlockSpec(memory_space=pltpu.VMEM)
    smem = pl.BlockSpec(memory_space=pltpu.SMEM)
    f32, bf16 = jnp.float32, jnp.bfloat16
    L = BLOCK_LEN
    dma = pltpu.SemaphoreType.DMA
    y_out, new_states = pl.pallas_call(
        functools.partial(layer_kernel, devices, blocks, owners),
        out_shape=(
            jax.ShapeDtypeStruct((tokens, columns), bf16),
            jax.ShapeDtypeStruct((devices * 16, state), bf16),
        ),
        in_specs=[smem] * 6 + [vmem] * 2 + [pl.BlockSpec(memory_space=pl.ANY)] * 4,
        out_specs=(vmem, vmem),
        scratch_shapes=[
            pltpu.VMEM((tokens, columns), bf16),
            pltpu.VMEM((tokens, columns), bf16),
            pltpu.VMEM((devices * 16, state), f32),
            pltpu.VMEM((2 * tokens, state), bf16),
            pltpu.VMEM((devices, 16, state), bf16),
            pltpu.VMEM((devices, 16, state), bf16),
            pltpu.VMEM((devices, 16, state), bf16),
            pltpu.VMEM((devices, 16, state), bf16),
            pltpu.VMEM((blocks, L), f32),
            pltpu.VMEM((4, blocks, L), f32),
            pltpu.VMEM((owners, L, state), f32),
            pltpu.VMEM((2 * blocks, L, L), f32),
            pltpu.VMEM((blocks, L, L), f32),
            pltpu.VMEM((blocks, L, state), f32),
            pltpu.VMEM((blocks, L, state), bf16),
            pltpu.VMEM((tokens, columns), bf16),
            pltpu.VMEM((tokens, columns), f32),
            pltpu.VMEM((4 * blocks, L), f32),
            pltpu.VMEM((L, L), f32),
            pltpu.VMEM((2 * blocks, L), f32),
            pltpu.VMEM((L, L), f32),
        ]
        + [dma((2, quads))] * 8
        + [dma((devices,))] * 4
        + [dma((4,))] * 2
        + [dma((5,))],
        compiler_params=pltpu.CompilerParams(
            collective_id=0, has_side_effects=True, vmem_limit_bytes=63 * 1024 * 1024
        ),
    )(
        owner_map,
        prefill_slot,
        turn_blocks,
        dt_bias,
        decay_rate,
        skip_d,
        dt_in,
        norm_gain.reshape(1, columns),
        x_in,
        z_in,
        bc_in,
        owner_states.reshape(-1, state),
    )
    return (y_out, new_states.astype(f32).reshape(owner_states.shape))


def choose(*arrays):
    x_in, dt_in, bc_in, owner_states, owner_map = (arrays[i] for i in (0, 2, 3, 4, 9))
    devices = lax.axis_size("dp")
    fits = (
        devices == 4 * bc_in.shape[0]
        and x_in.shape[0] == 16 * BLOCK_LEN
        and x_in.shape[1] == BLOCK_LEN
        and dt_in.shape[0] == 2
        and owner_states.shape[1] == 1
        and owner_states.shape[3] == 8
        and devices == 8 * owner_map.shape[0]
    )
    return (fused if fits else shards)(*arrays)


def solution(mesh):
    placed = (
        P("groups", "dp"),
        P("groups", "dp"),
        P("dp", "groups"),
        P(None, ("groups", "dp"), None),
        P(("groups", "dp"), None, None, None, None),
        P("dp"),
        P("dp"),
        P("dp"),
        P("dp"),
        P("groups"),
        P("groups"),
        P("groups"),
    )
    return jax.shard_map(
        choose,
        mesh=mesh,
        in_specs=placed,
        out_specs=(P("groups", "dp"), P(("groups", "dp"), None, None, None, None)),
        check_vma=False,
    )
```
